512 devices in a mesh: site: 32 (over z, core), mode: 16 (over y, x).
Axes of the slice: x: 4, y: 4, z: 16, core: 2. Of those that a mesh axis runs over, the one named last changes fastest.
Arguments:
- vectors: bfloat16 [2, 512, 147456], P(None, 'mode', 'site'), may hold values from -6 to 6
- images: bfloat16 [2, 512, 147456], P(None, 'mode', 'site'), may hold values from -0.02734375 to 0.02734375
- ritz: float32 [2, 512, 512], replicated, may hold values from -0.1875 to 0.1875
Outputs:
- rotated: bfloat16 [2, 512, 147456], P(None, 'mode', 'site')
- projected: float32 [2, 512, 512], replicated
The draws below stay inside these ranges and needn't reach their ends.
All inputs are finite; a program needn't handle non-finite values.
Results may differ from the reference program's by a relative error of at most 0.0049.
Values may be sent and summed in bfloat16 or wider, within the bound.
No kernel may reach another device: no remote copies, remote signals or barrier semaphores. Data moves between devices by JAX's collectives and lax.ppermute only.
A program may use at most 64 MiB of HBM per device.

```python
import jax
import jax.numpy as jnp
from jax import lax

NEV = 512
COMP = 147456


def levels(rng, shape, split, smallest, largest):
    loudness, own = 1.0, jax.random.fold_in(rng, 6)
    for axis_at, blocks in split:
        heights = jnp.exp(jax.random.uniform(jax.random.fold_in(own, axis_at), (blocks,), jnp.float32, smallest / len(split), largest / len(split)))
        loudness = loudness * jnp.repeat(heights, shape[axis_at] // blocks).reshape([-1 if axis == axis_at else 1 for axis in range(len(shape))])
    return loudness


def scatter_about(key, extent, spread, limit, cuts=(), dtype=jnp.bfloat16):
    values = jax.random.normal(key, extent, jnp.float32) * spread
    if len(cuts) > 0:
        values = levels(key, extent, cuts, -0.22, 0.18) * values
    return jnp.clip(values, min=-limit, max=limit).astype(dtype)


def setup_inputs(seed: int = 0) -> dict:
    keys = jax.random.split(jax.random.key(seed), 4)
    return {
        "vectors": scatter_about(keys[0], (2, NEV, COMP), 1.0, 6.0, ((1, 16), (2, 32))),
        "images": scatter_about(keys[1], (2, NEV, COMP), ((2 * COMP) ** -0.5), 0.02734375, ((1, 16), (2, 32))),
        "ritz": scatter_about(keys[2], (2, NEV, NEV), (2 * NEV) ** -0.5, 0.1875, (), jnp.float32),
    }


def stacked_ritz(coeffs):
    upper = jnp.concatenate([coeffs[0], coeffs[1]], axis=1)
    lower = jnp.concatenate([-coeffs[1], coeffs[0]], axis=1)
    return jnp.concatenate([upper, lower], axis=0)


def gram_blocks(left_rows, right_rows, left_count, right_count):
    products = lax.dot_general(left_rows, right_rows, (((1,), (1,)), ((), ())), preferred_element_type=jnp.float32)
    real_part = products[:left_count, :right_count] + products[left_count:, right_count:]
    imag_part = products[:left_count, right_count:] - products[left_count:, :right_count]
    return jnp.stack([real_part, imag_part])


def highest_dot(first_matrix, second_matrix):
    return jnp.dot(first_matrix, second_matrix, precision=lax.Precision.HIGHEST, preferred_element_type=jnp.float32)


def project(gram, left_coeffs, right_coeffs):
    mixed_re = highest_dot(gram[0], right_coeffs[0]) - highest_dot(gram[1], right_coeffs[1])
    mixed_im = highest_dot(gram[0], right_coeffs[1]) + highest_dot(gram[1], right_coeffs[0])
    result_re = highest_dot(left_coeffs[0].T, mixed_re) + highest_dot(left_coeffs[1].T, mixed_im)
    result_im = highest_dot(left_coeffs[0].T, mixed_im) - highest_dot(left_coeffs[1].T, mixed_re)
    return jnp.stack([result_re, result_im])


def reference(vectors, images, ritz):
    ritz_low = ritz.astype(jnp.bfloat16)
    vector_rows = vectors.reshape(2 * NEV, COMP)
    image_rows = images.reshape(2 * NEV, COMP)
    rotated = lax.dot_general(stacked_ritz(ritz_low), vector_rows, (((0,), (0,)), ((), ())), preferred_element_type=jnp.float32)
    rotated = rotated.astype(jnp.bfloat16).reshape(2, NEV, COMP)
    gram = gram_blocks(vector_rows, image_rows, NEV, NEV)
    projected = project(gram, ritz, ritz)
    return rotated, projected
```

```python
import functools

import jax
import jax.numpy as jnp
from jax import lax
from jax.experimental import pallas as pl
from jax.experimental.pallas import tpu as pltpu
from jax.sharding import PartitionSpec as P

BF16 = jnp.bfloat16
F32 = jnp.float32
LANES = 128
VMEM_BYTES = 48 * 1024 * 1024

PEERS = 16
OWNED = 32
MODES = PEERS * OWNED
MAIN = 2 * LANES
QUARTER = LANES // 4
TAIL_AT = PEERS * MAIN
ROTATED_ROWS = 144
SHARE_ROWS = 256
PLANES = 4

NT = (((1,), (1,)), ((), ()))


def lane_group(shape):
    return lax.broadcasted_iota(jnp.int32, shape, len(shape) - 1) // QUARTER


def pack_kernel(vectors_ref, images_ref, out_ref):
    sources = (vectors_ref, images_ref)
    for peer in range(PEERS):
        for which, source in enumerate(sources):
            for half in range(2):
                at = peer * MAIN + half * LANES
                for part in range(2):
                    row = ((which * 2 + half) * 2 + part) * OWNED
                    out_ref[peer, row : row + OWNED, :] = source[part, :, at : at + LANES]
    group = lane_group((OWNED, LANES))
    for block in range(PEERS // 4):
        at = TAIL_AT + block * LANES
        tails = [sources[which][part, :, at : at + LANES].astype(F32) for part in range(2) for which in range(2)]
        for quarter in range(4):
            packed = jnp.zeros((OWNED, LANES), F32)
            for slot, tail in enumerate(tails):
                shift = (slot - quarter) % 4 * QUARTER
                moved = pltpu.roll(tail, shift, 1) if shift else tail
                packed = jnp.where(group == slot, moved, packed)
            out_ref[block * 4 + quarter, 8 * OWNED : 9 * OWNED, :] = packed.astype(BF16)


def coefficients_kernel(ritz_ref, high_ref, low_ref):
    real, imag = ritz_ref[0].T, ritz_ref[1].T
    for row, column, block in ((0, 0, real), (0, 1, -imag), (1, 0, imag), (1, 1, real)):
        high = block.astype(BF16)
        rows, columns = pl.ds(row * MODES, MODES), pl.ds(column * MODES, MODES)
        high_ref[rows, columns] = high
        low_ref[rows, columns] = (block - high.astype(F32)).astype(BF16)


def split(values):
    high = values.astype(BF16)
    return high, (values - high.astype(F32)).astype(BF16)


def local_kernel(got_ref, high_ref, low_ref, out_ref, stacked, tail, left, right):
    for part in range(2):
        rows = slice(part * MODES, (part + 1) * MODES)
        for block in range(4):
            at = (block * 2 + part) * OWNED
            stacked[rows, block * LANES : (block + 1) * LANES] = got_ref[:, at : at + OWNED, :].reshape(MODES, LANES)
    packed = got_ref[:, 8 * OWNED : 9 * OWNED, :].reshape(MODES, LANES)
    stacked[0:MODES, 4 * LANES : 5 * LANES] = packed
    stacked[MODES : 2 * MODES, 4 * LANES : 5 * LANES] = pltpu.roll(packed.astype(F32), 2 * QUARTER, 1).astype(BF16)

    tile = 256
    group = lane_group((tile, LANES))
    for step in range(2 * MODES // tile):
        part, at = divmod(step * tile, MODES)
        rows = slice(step * tile, (step + 1) * tile)
        rotated = jnp.dot(high_ref[rows, :], stacked[...], preferred_element_type=F32)
        for block in range(2):
            values = rotated[:, block * LANES : (block + 1) * LANES].astype(BF16).reshape(tile // OWNED, OWNED, LANES)
            row = (block * 2 + part) * OWNED
            out_ref[at // OWNED : (at + tile) // OWNED, row : row + OWNED, :] = values
        tail[rows, :] = rotated[:, 4 * LANES : 5 * LANES]
        exact = rotated + jnp.dot(low_ref[rows, :], stacked[...], preferred_element_type=F32)
        here = slice(at, at + tile)
        for side, target in enumerate((left, right)):
            for index, values in enumerate(split(exact[:, side * MAIN : (side + 1) * MAIN])):
                target[index, here, part * MAIN : (part + 1) * MAIN] = values
            ends = exact[:, 4 * LANES : 5 * LANES]
            shift = (part - side) % 4 * QUARTER
            ends = pltpu.roll(ends, shift, 1) if shift else ends
            if part == 0:
                ends = jnp.where(group == 0, ends, 0.0)
            else:
                ends = jnp.where(group == 1, ends, 0.0)
            for index, values in enumerate(split(ends)):
                columns = slice(2 * MAIN, 2 * MAIN + LANES)
                if part == 0:
                    target[index, here, columns] = values
                else:
                    target[index, here, columns] = target[index, here, columns] + values

    group = lane_group((PEERS, 16, LANES))
    quarters = [tail[part * MODES : (part + 1) * MODES, :].reshape(PEERS, OWNED, LANES)[:, 16 * half : 16 * half + 16, :]
                for part in range(2) for half in range(2)]
    ends = quarters[0]
    for slot in range(1, 4):
        ends = jnp.where(group == slot, pltpu.roll(quarters[slot], slot * QUARTER, 2), ends)
    out_ref[:, 4 * OWNED : 4 * OWNED + 16, :] = ends.astype(BF16)

    for column in range(4):
        here = slice(column * LANES, (column + 1) * LANES)
        group = lane_group((LANES, LANES))
        real, imag = [], []
        for index in range(2):
            re = right[index, here, 0:MAIN]
            im = right[index, here, MAIN : 2 * MAIN]
            ends = right[index, here, 2 * MAIN : 2 * MAIN + LANES].astype(F32)
            swapped = jnp.where(group == 0, pltpu.roll(ends, LANES - QUARTER, 1), -pltpu.roll(ends, QUARTER, 1))
            swapped = jnp.where(group < 2, swapped, 0.0)
            real.append(right[index, here, :])
            imag.append(jnp.concatenate([im, -re, swapped.astype(BF16)], axis=1))
        for part, sides in enumerate((real, imag)):
            share = lax.dot_general(left[0], sides[0], NT, preferred_element_type=F32)
            share += lax.dot_general(left[0], sides[1], NT, preferred_element_type=F32)
            share += lax.dot_general(left[1], sides[0], NT, preferred_element_type=F32)
            row = ROTATED_ROWS + (column * 2 + part) * OWNED
            out_ref[:, row : row + OWNED, :] = share.astype(BF16).reshape(PEERS, OWNED, LANES)


def unpack_kernel(back_ref, out_ref):
    for peer in range(PEERS):
        for half in range(2):
            at = peer * MAIN + half * LANES
            for part in range(2):
                row = (half * 2 + part) * OWNED
                out_ref[part, :, at : at + LANES] = back_ref[peer, row : row + OWNED, :]
    group = lane_group((16, LANES))
    for block in range(PEERS // 4):
        ends = [back_ref[block * 4 + quarter, 4 * OWNED : 4 * OWNED + 16, :].astype(F32) for quarter in range(4)]
        at = TAIL_AT + block * LANES
        for slot in range(4):
            values = jnp.zeros((16, LANES), F32)
            for quarter, end in enumerate(ends):
                shift = (quarter - slot) % 4 * QUARTER
                moved = pltpu.roll(end, shift, 1) if shift else end
                values = jnp.where(group == quarter, moved, values)
            part, half = divmod(slot, 2)
            out_ref[part, 16 * half : 16 * half + 16, at : at + LANES] = values.astype(BF16)


def widen_kernel(pieces_ref, out_ref):
    for peer in range(PEERS):
        for column in range(4):
            for part in range(2):
                row = (column * 2 + part) * OWNED
                out_ref[part, peer * OWNED : (peer + 1) * OWNED, column * LANES : (column + 1) * LANES] = pieces_ref[
                    peer, row : row + OWNED, :
                ].astype(F32)


def call(kernel, name, outs, *args, flops=0, scratch=()):
    outs = tuple(jax.ShapeDtypeStruct(shape, dtype) for shape, dtype in outs)
    moved = sum(a.size * a.dtype.itemsize for a in args + outs)
    return pl.pallas_call(
        kernel,
        name=name,
        out_shape=outs if len(outs) > 1 else outs[0],
        in_specs=[pl.BlockSpec(memory_space=pltpu.VMEM)] * len(args),
        out_specs=(
            [pl.BlockSpec(memory_space=pltpu.VMEM)] * len(outs)
            if len(outs) > 1
            else pl.BlockSpec(memory_space=pltpu.VMEM)
        ),
        scratch_shapes=list(scratch),
        cost_estimate=pl.CostEstimate(flops=flops, bytes_accessed=moved, transcendentals=0),
        compiler_params=pltpu.CompilerParams(vmem_limit_bytes=VMEM_BYTES),
    )(*args)


def exchange(pieces, axis, groups=None):
    return lax.all_to_all(pieces, axis, 0, 0, axis_index_groups=groups)


def spread(piece, count, axis, groups=None):
    return exchange(jnp.broadcast_to(piece[None], (count,) + piece.shape), axis, groups)


def on_device(site_count, vectors, images, ritz):
    near = 2 * PLANES
    far = site_count // near
    near_groups = [[near * h + i for i in range(near)] for h in range(far)]
    far_groups = [[near * h + i for h in range(far)] for i in range(near)]

    high, low = call(
        coefficients_kernel, "coefficients", [((2 * MODES, 2 * MODES), BF16)] * 2, ritz
    )
    packed = call(pack_kernel, "pack", [((PEERS, 9 * OWNED, LANES), BF16)], vectors, images)
    got = exchange(packed, "mode")
    shares = call(
        local_kernel,
        "rotate_and_project",
        [((PEERS, ROTATED_ROWS + SHARE_ROWS, LANES), BF16)],
        got,
        high,
        low,
        flops=5 * 10**9,
        scratch=[
            pltpu.VMEM((2 * MODES, 5 * LANES), BF16),
            pltpu.VMEM((2 * MODES, LANES), F32),
            pltpu.VMEM((2, MODES, 5 * LANES), BF16),
            pltpu.VMEM((2, MODES, 5 * LANES), BF16),
        ],
    )
    back = exchange(shares, "mode")
    rotated = call(unpack_kernel, "unpack", [((2, OWNED, PEERS * MAIN + 4 * LANES), BF16)], back)

    summed = jnp.sum(back[:, ROTATED_ROWS:, :].astype(F32), axis=0)
    summed = jnp.sum(exchange(summed.reshape(near, OWNED, LANES), "site", near_groups), axis=0)
    summed = jnp.sum(spread(summed, far, "site", far_groups), axis=0)
    rows = spread(summed.astype(BF16), near, "site", near_groups)
    pieces = spread(rows.reshape(SHARE_ROWS, LANES), PEERS, "mode")
    projected = call(widen_kernel, "widen", [((2, MODES, MODES), F32)], pieces)
    return rotated, projected


def solution(mesh):
    placed = (P(None, "mode", "site"), P(None, "mode", "site"), P())
    return jax.shard_map(
        functools.partial(on_device, mesh.shape["site"]),
        mesh=mesh,
        in_specs=placed,
        out_specs=(P(None, "mode", "site"), P()),
        check_vma=False,
    )
```

```python
import functools

import jax
import jax.numpy as jnp
from jax import lax
from jax.experimental import pallas as pl
from jax.experimental.pallas import tpu as pltpu
from jax.sharding import PartitionSpec as P

BF16 = jnp.bfloat16
F32 = jnp.float32
LANES = 128
MIB = 1024 * 1024

PEERS = 16
OWNED = 32
HALF = OWNED // 2
MODES = PEERS * OWNED
HALF_MODES = MODES // 2
MAIN = 2 * LANES
QUARTER = LANES // 4
TAIL_AT = PEERS * MAIN
TAIL_ROW = 4 * OWNED
PIECE_ROWS = TAIL_ROW + HALF
DEPTH = 2 * MAIN + LANES
SHARE_ROWS = 8 * HALF
CHUNKS = 4
NEAR = 4
ROWS = HALF // NEAR

NT = (((1,), (1,)), ((), ()))


def lane_group(shape):
    return lax.broadcasted_iota(jnp.int32, shape, len(shape) - 1) // QUARTER


def turn(values, groups):
    shift = groups % 4 * QUARTER
    return pltpu.roll(values, shift, len(values.shape) - 1) if shift else values


def pack_kernel(vectors_hbm, images_hbm, out_hbm, vectors_ref, images_ref, out_ref, arrived, sent):
    peers = PEERS // CHUNKS
    copies = []
    for which, (source, target) in enumerate(((vectors_hbm, vectors_ref), (images_hbm, images_ref))):
        for chunk in range(CHUNKS + 1):
            at = chunk * peers * MAIN
            lanes = pl.ds(at, TAIL_AT // CHUNKS if chunk < CHUNKS else 4 * LANES)
            copy = pltpu.make_async_copy(
                source.at[:, :, lanes], target.at[:, :, lanes], arrived.at[which * (CHUNKS + 1) + chunk]
            )
            copy.start()
            copies.append(copy)
    group = lane_group((HALF, LANES))
    leaving = []
    for which, source_ref in enumerate((vectors_ref, images_ref)):
        base = which * PIECE_ROWS
        for chunk in range(CHUNKS + 1):
            index = which * (CHUNKS + 1) + chunk
            copies[index].wait()
            if chunk < CHUNKS:
                for peer in range(chunk * peers, (chunk + 1) * peers):
                    for block in range(2):
                        at = peer * MAIN + block * LANES
                        for part in range(2):
                            row = base + (block * 2 + part) * OWNED
                            out_ref[peer, row : row + OWNED, :] = source_ref[part, :, at : at + LANES]
                where = (pl.ds(chunk * peers, peers), pl.ds(base, TAIL_ROW))
            else:
                for block in range(PEERS // 4):
                    at = TAIL_AT + block * LANES
                    tails = [
                        source_ref[part, half * HALF : (half + 1) * HALF, at : at + LANES].astype(F32)
                        for part in range(2)
                        for half in range(2)
                    ]
                    for quarter in range(4):
                        packed = turn(tails[0], -quarter)
                        for slot in range(1, 4):
                            packed = jnp.where(group == slot, turn(tails[slot], slot - quarter), packed)
                        out_ref[block * 4 + quarter, base + TAIL_ROW : base + PIECE_ROWS, :] = packed.astype(BF16)
                where = (pl.ds(0, PEERS), pl.ds(base + TAIL_ROW, HALF))
            copy = pltpu.make_async_copy(out_ref.at[where], out_hbm.at[where], sent.at[index])
            copy.start()
            leaving.append(copy)
    for copy in leaving:
        copy.wait()


def unpack_kernel(back_ref, out_ref):
    for peer in range(PEERS):
        for block in range(2):
            at = peer * MAIN + block * LANES
            for part in range(2):
                row = SHARE_ROWS + (block * 2 + part) * OWNED
                out_ref[part, :, at : at + LANES] = back_ref[peer, row : row + OWNED, :]
    group = lane_group((HALF, LANES))
    for block in range(PEERS // 4):
        ends = [back_ref[block * 4 + quarter, SHARE_ROWS + TAIL_ROW : SHARE_ROWS + PIECE_ROWS, :].astype(F32) for quarter in range(4)]
        at = TAIL_AT + block * LANES
        for slot in range(4):
            values = turn(ends[0], -slot)
            for quarter in range(1, 4):
                values = jnp.where(group == quarter, turn(ends[quarter], quarter - slot), values)
            part, half = divmod(slot, 2)
            out_ref[part, half * HALF : (half + 1) * HALF, at : at + LANES] = values.astype(BF16)


def split(values):
    high = values.astype(BF16)
    return high, (values - high.astype(F32)).astype(BF16)


def turn_kernel(ritz_ref, turn_ref):
    real, imag = ritz_ref[0].T, ritz_ref[1].T
    for row, column, block in ((0, 0, real), (0, 1, -imag), (1, 0, imag), (1, 1, real)):
        turn_ref[row * MODES : (row + 1) * MODES, column * MODES : (column + 1) * MODES] = block.astype(BF16)


def split_kernel(ritz_ref, high_ref, low_ref):
    for part in range(2):
        high_ref[part], low_ref[part] = split(ritz_ref[part])


def left_kernel(ritz_ref, left_high_ref, left_low_ref):
    groups = (PEERS, 2, HALF // 8, 8, MODES)
    first = lax.broadcasted_iota(jnp.int32, (PEERS, 8, MODES), 1) < ROWS
    real, imag = ritz_ref[0].reshape(groups), ritz_ref[1].reshape(groups)
    for core in range(2):
        for part in range(2):
            blocks = []
            for pair in range(HALF // 8):
                one, two = (real, imag) if part == 0 else (-imag, real)
                one, two = one[:, core, pair], two[:, core, pair]
                blocks.append(jnp.where(first, one, pltpu.roll(two, ROWS, 1)))
                blocks.append(jnp.where(first, pltpu.roll(one, ROWS, 1), two))
            values = jnp.concatenate(blocks, axis=1).reshape(MODES, MODES).T
            rows = slice(part * MODES, (part + 1) * MODES)
            left_high_ref[core, rows, :], left_low_ref[core, rows, :] = split(values)


def rotate_kernel(got_ref, turn_ref, out_ref, stacked):
    packed = got_ref[:, TAIL_ROW:PIECE_ROWS, :].astype(F32)
    for part in range(2):
        rows = slice(part * MODES, (part + 1) * MODES)
        for block in range(2):
            at = (block * 2 + part) * OWNED
            stacked[rows, block * LANES : (block + 1) * LANES] = got_ref[:, at : at + OWNED, :].reshape(MODES, LANES)
        ends = jnp.concatenate([turn(packed, -2 * part), turn(packed, -2 * part - 1)], axis=1)
        stacked[rows, MAIN : MAIN + LANES] = ends.reshape(MODES, LANES).astype(BF16)

    owners = HALF_MODES // OWNED
    group = lane_group((owners, HALF, LANES))
    for step in range(2):
        peers = slice(step * owners, (step + 1) * owners)
        sent = None
        for part in range(2):
            at = part * MODES + step * HALF_MODES
            rotated = jnp.dot(turn_ref[at : at + HALF_MODES, :], stacked[...], preferred_element_type=F32)
            for block in range(2):
                row = (block * 2 + part) * OWNED
                values = rotated[:, block * LANES : (block + 1) * LANES].astype(BF16)
                out_ref[peers, row : row + OWNED, :] = values.reshape(owners, OWNED, LANES)
            ends = rotated[:, MAIN : MAIN + LANES].reshape(owners, OWNED, LANES)
            for half in range(2):
                moved = turn(ends[:, half * HALF : (half + 1) * HALF, :], part * 2 + half)
                sent = moved if sent is None else jnp.where(group == part * 2 + half, moved, sent)
        out_ref[peers, TAIL_ROW:PIECE_ROWS, :] = sent.astype(BF16)


def share_kernel(other, got_ref, out_ref, left, right):
    core = lax.rem(lax.axis_index("site"), 2)
    half = 1 - core if other else core
    group = lane_group((PEERS, HALF, LANES))

    def side(packed, row_half, sources, signs):
        first, second = (turn(packed, place - 2 * sources[place] - row_half) * signs[place] for place in range(2))
        return jnp.where(group == 0, first, jnp.where(group == 1, second, 0.0))

    packed = got_ref[:, TAIL_ROW:PIECE_ROWS, :].astype(F32)
    for part in range(2):
        for block in range(2):
            row = pl.multiple_of((block * 2 + part) * OWNED + half * HALF, HALF)
            at = part * MAIN + block * LANES
            left[:, at : at + LANES] = got_ref[:, pl.ds(row, HALF), :].reshape(HALF_MODES, LANES)
    ends = jnp.where(half == 0, side(packed, 0, (0, 1), (1, 1)), side(packed, 1, (0, 1), (1, 1)))
    left[:, 2 * MAIN : DEPTH] = ends.reshape(HALF_MODES, LANES).astype(BF16)

    packed = got_ref[:, PIECE_ROWS + TAIL_ROW : 2 * PIECE_ROWS, :].astype(F32)
    for part in range(2):
        sources, signs = ((0, 1), (1, 1)) if part == 0 else ((1, 0), (1, -1))
        for place in range(2):
            for block in range(2):
                at = PIECE_ROWS + (block * 2 + sources[place]) * OWNED
                values = got_ref[:, at : at + OWNED, :].reshape(MODES, LANES)
                lanes = slice(place * MAIN + block * LANES, place * MAIN + (block + 1) * LANES)
                right[part, :, lanes] = values if signs[place] > 0 else -values
        ends = jnp.concatenate([side(packed, row_half, sources, signs) for row_half in range(2)], axis=1)
        right[part, :, 2 * MAIN : DEPTH] = ends.reshape(MODES, LANES).astype(BF16)
    for part in range(2):
        share = lax.dot_general(left[...], right[part], NT, preferred_element_type=F32)
        for column in range(4):
            row = (part * 4 + column) * HALF
            values = share[:, column * LANES : (column + 1) * LANES].reshape(PEERS, HALF, LANES)
            out_ref[:, row : row + HALF, :] = values.astype(out_ref.dtype)


def assemble_kernel(kept_ref, taken_ref, turned_ref, out_ref):
    out_ref[:, 0:SHARE_ROWS, :] = (kept_ref[...] + taken_ref[...].astype(F32)).astype(BF16)
    out_ref[:, SHARE_ROWS:, :] = turned_ref[...]


def sum_kernel(back_ref, out_ref):
    total = back_ref[0, 0:SHARE_ROWS, :].astype(F32)
    for peer in range(1, PEERS):
        total += back_ref[peer, 0:SHARE_ROWS, :].astype(F32)
    for part in range(2):
        for column in range(4):
            at = (part * 4 + column) * HALF
            for near in range(NEAR):
                out_ref[near, part * ROWS : (part + 1) * ROWS, column * LANES : (column + 1) * LANES] = total[
                    at + near * ROWS : at + (near + 1) * ROWS, :
                ]


def project_kernel(far_ref, high_ref, low_ref, out_ref):
    total = far_ref[0]
    for peer in range(1, far_ref.shape[0]):
        total += far_ref[peer]
    high, low = split(total)
    both = jnp.concatenate([high.astype(F32), low.astype(F32)], axis=0).astype(BF16)
    products = []
    for part in range(2):
        first = jnp.dot(both, high_ref[part], preferred_element_type=F32)
        second = jnp.dot(both, low_ref[part], preferred_element_type=F32)
        products.append(first[0 : 2 * ROWS] + first[2 * ROWS : 4 * ROWS] + second[0 : 2 * ROWS])
    real = products[0][0:ROWS] - products[1][ROWS : 2 * ROWS]
    imag = products[0][ROWS : 2 * ROWS] + products[1][0:ROWS]
    rows = jnp.concatenate([real, imag], axis=0)
    for near in range(NEAR):
        out_ref[near] = rows


def finish_products(half, rows_ref, high_ref, low_ref, here):
    rows = rows_ref[...].reshape(MODES, MODES)
    total = jnp.dot(high_ref[half, here, :], rows, preferred_element_type=F32)
    return total + jnp.dot(low_ref[half, here, :], rows, preferred_element_type=F32)


def finish_own_kernel(rows_ref, high_ref, low_ref, out_ref):
    core = lax.rem(lax.axis_index("site"), 2)
    for part in range(2):
        out_ref[part] = finish_products(core, rows_ref, high_ref, low_ref, pl.ds(part * MODES, MODES))


def finish_other_kernel(rows_ref, high_ref, low_ref, first_ref, out_hbm, total, sent):
    core = lax.rem(lax.axis_index("site"), 2)
    copies = []
    for part in range(2):
        for half in range(2):
            rows = pl.ds(half * HALF_MODES, HALF_MODES)
            here = pl.ds(part * MODES + half * HALF_MODES, HALF_MODES)
            total[part, rows, :] = first_ref[part, rows, :] + finish_products(1 - core, rows_ref, high_ref, low_ref, here)
            copy = pltpu.make_async_copy(total.at[part, rows, :], out_hbm.at[part, rows, :], sent.at[part * 2 + half])
            copy.start()
            copies.append(copy)
    for copy in copies:
        copy.wait()


def call(kernel, name, outs, *args, flops=0, scratch=(), in_place=False, out_place=False, vmem=16):
    outs = tuple(jax.ShapeDtypeStruct(shape, dtype) for shape, dtype in outs)
    moved = sum(a.size * a.dtype.itemsize for a in args + outs)
    whole = pl.BlockSpec(memory_space=pltpu.VMEM)
    source = pl.BlockSpec(memory_space=pltpu.HBM) if in_place else whole
    target = pl.BlockSpec(memory_space=pltpu.HBM) if out_place else whole
    single = len(outs) == 1
    return pl.pallas_call(
        kernel,
        name=name,
        out_shape=outs[0] if single else outs,
        in_specs=[source] * len(args),
        out_specs=target if single else [target] * len(outs),
        scratch_shapes=list(scratch),
        cost_estimate=pl.CostEstimate(flops=flops, bytes_accessed=moved, transcendentals=0),
        compiler_params=pltpu.CompilerParams(vmem_limit_bytes=vmem * MIB),
    )(*args)


def exchange(pieces, axis, groups=None):
    return lax.all_to_all(pieces, axis, 0, 0, axis_index_groups=groups)


def spread(piece, count):
    return jnp.broadcast_to(piece[None], (count,) + piece.shape)


def on_device(site_count, vectors, images, ritz):
    far = site_count // (2 * NEAR)
    near_groups = [[2 * (NEAR * h + z) + c for z in range(NEAR)] for h in range(far) for c in range(2)]
    far_groups = [[2 * (NEAR * h + z) + c for h in range(far)] for z in range(NEAR) for c in range(2)]
    swap = [(i, i ^ 1) for i in range(site_count)]
    width = PEERS * MAIN + 4 * LANES
    share = (PEERS, SHARE_ROWS, LANES)
    square = (2 * MODES, 2 * MODES)
    local = [((2, OWNED, width), BF16)]

    packed = call(
        pack_kernel,
        "pack",
        [((PEERS, 2 * PIECE_ROWS, LANES), BF16)],
        vectors,
        images,
        scratch=[
            pltpu.VMEM((2, OWNED, width), BF16),
            pltpu.VMEM((2, OWNED, width), BF16),
            pltpu.VMEM((PEERS, 2 * PIECE_ROWS, LANES), BF16),
            pltpu.SemaphoreType.DMA((2 * CHUNKS + 2,)),
            pltpu.SemaphoreType.DMA((2 * CHUNKS + 2,)),
        ],
        in_place=True,
        out_place=True,
        vmem=60,
    )
    packed, ritz = lax.optimization_barrier((packed, ritz))
    factors = (
        call(turn_kernel, "turn_matrix", [(square, BF16)], ritz),
        call(left_kernel, "left_factors", [((2, 2 * MODES, MODES), BF16)] * 2, ritz),
        call(split_kernel, "split_ritz", [(ritz.shape, BF16)] * 2, ritz),
    )
    got, (turn_matrix, left, ritz_split) = lax.optimization_barrier((exchange(packed, "mode"), factors))

    sides = [pltpu.VMEM((HALF_MODES, DEPTH), BF16), pltpu.VMEM((2, MODES, DEPTH), BF16)]
    given = call(functools.partial(share_kernel, True), "share_given", [(share, BF16)], got, flops=10**9, scratch=sides)
    taken = lax.ppermute(given, "site", swap)
    kept = call(functools.partial(share_kernel, False), "share_kept", [(share, F32)], got, flops=10**9, scratch=sides)
    turned = call(
        rotate_kernel,
        "rotate",
        [((PEERS, PIECE_ROWS, LANES), BF16)],
        got,
        turn_matrix,
        flops=10**9,
        scratch=[pltpu.VMEM((2 * MODES, MAIN + LANES), BF16)],
    )
    sent = call(assemble_kernel, "assemble", [((PEERS, SHARE_ROWS + PIECE_ROWS, LANES), BF16)], kept, taken, turned)
    back = exchange(sent, "mode")
    summed = call(sum_kernel, "sum_shares", [((NEAR, 2 * ROWS, MODES), F32)], back)
    summed = exchange(summed, "site", near_groups)
    summed = exchange(spread(jnp.sum(summed, axis=0), far), "site", far_groups)
    rows = call(project_kernel, "project", [((NEAR, 2 * ROWS, MODES), F32)], summed, *ritz_split)
    rows = exchange(rows, "site", near_groups).reshape(OWNED, MODES).astype(BF16)
    own = exchange(spread(rows, PEERS), "mode")
    own, back = lax.optimization_barrier((own, back))
    other = lax.ppermute(own, "site", swap)
    rotated = call(unpack_kernel, "unpack", local, back)
    whole = [((2, MODES, MODES), F32)]
    first = call(finish_own_kernel, "finish_own", whole, own, *left, flops=10**9)
    projected = call(
        finish_other_kernel,
        "finish_other",
        whole,
        other,
        *left,
        first,
        flops=10**9,
        scratch=[pltpu.VMEM((2, MODES, MODES), F32), pltpu.SemaphoreType.DMA((4,))],
        out_place=True,
    )
    return rotated, projected


def solution(mesh):
    placed = (P(None, "mode", "site"), P(None, "mode", "site"), P())
    return jax.shard_map(
        functools.partial(on_device, mesh.shape["site"]),
        mesh=mesh,
        in_specs=placed,
        out_specs=(P(None, "mode", "site"), P()),
        check_vma=False,
    )
```

```python
import functools

import jax
import jax.numpy as jnp
from jax import lax
from jax.experimental import pallas as pl
from jax.experimental.pallas import tpu as pltpu
from jax.sharding import PartitionSpec as P

BF16 = jnp.bfloat16
F32 = jnp.float32
LANES = 128
MIB = 1024 * 1024

PEERS = 16
OWNED = 32
HALF = OWNED // 2
MODES = PEERS * OWNED
HALF_MODES = MODES // 2
MAIN = 2 * LANES
QUARTER = LANES // 4
TAIL_AT = PEERS * MAIN
TAIL_ROW = 4 * OWNED
PIECE_ROWS = TAIL_ROW + HALF
DEPTH = 2 * MAIN + LANES
SHARE_ROWS = 8 * HALF
CHUNKS = 4
NEAR = 4

NT = (((1,), (1,)), ((), ()))


def lane_group(shape):
    return lax.broadcasted_iota(jnp.int32, shape, len(shape) - 1) // QUARTER


def turn(values, groups):
    shift = groups % 4 * QUARTER
    return pltpu.roll(values, shift, len(values.shape) - 1) if shift else values


def pack_kernel(vectors_hbm, images_hbm, out_hbm, vectors_ref, images_ref, out_ref, arrived, sent):
    peers = PEERS // CHUNKS
    copies = []
    for which, (source, target) in enumerate(((vectors_hbm, vectors_ref), (images_hbm, images_ref))):
        for chunk in range(CHUNKS + 1):
            at = chunk * peers * MAIN
            lanes = pl.ds(at, TAIL_AT // CHUNKS if chunk < CHUNKS else 4 * LANES)
            copy = pltpu.make_async_copy(
                source.at[:, :, lanes], target.at[:, :, lanes], arrived.at[which * (CHUNKS + 1) + chunk]
            )
            copy.start()
            copies.append(copy)
    group = lane_group((HALF, LANES))
    leaving = []
    for which, source_ref in enumerate((vectors_ref, images_ref)):
        base = which * PIECE_ROWS
        for chunk in range(CHUNKS + 1):
            index = which * (CHUNKS + 1) + chunk
            copies[index].wait()
            if chunk < CHUNKS:
                for peer in range(chunk * peers, (chunk + 1) * peers):
                    for block in range(2):
                        at = peer * MAIN + block * LANES
                        for part in range(2):
                            row = base + (block * 2 + part) * OWNED
                            out_ref[peer, row : row + OWNED, :] = source_ref[part, :, at : at + LANES]
                where = (pl.ds(chunk * peers, peers), pl.ds(base, TAIL_ROW))
            else:
                for block in range(PEERS // 4):
                    at = TAIL_AT + block * LANES
                    tails = [
                        source_ref[part, half * HALF : (half + 1) * HALF, at : at + LANES].astype(F32)
                        for part in range(2)
                        for half in range(2)
                    ]
                    for quarter in range(4):
                        packed = turn(tails[0], -quarter)
                        for slot in range(1, 4):
                            packed = jnp.where(group == slot, turn(tails[slot], slot - quarter), packed)
                        out_ref[block * 4 + quarter, base + TAIL_ROW : base + PIECE_ROWS, :] = packed.astype(BF16)
                where = (pl.ds(0, PEERS), pl.ds(base + TAIL_ROW, HALF))
            copy = pltpu.make_async_copy(out_ref.at[where], out_hbm.at[where], sent.at[index])
            copy.start()
            leaving.append(copy)
    for copy in leaving:
        copy.wait()


def unpack_kernel(back_ref, out_ref):
    for peer in range(PEERS):
        for block in range(2):
            at = peer * MAIN + block * LANES
            for part in range(2):
                row = SHARE_ROWS + (block * 2 + part) * OWNED
                out_ref[part, :, at : at + LANES] = back_ref[peer, row : row + OWNED, :]
    group = lane_group((HALF, LANES))
    for block in range(PEERS // 4):
        ends = [back_ref[block * 4 + quarter, SHARE_ROWS + TAIL_ROW : SHARE_ROWS + PIECE_ROWS, :].astype(F32) for quarter in range(4)]
        at = TAIL_AT + block * LANES
        for slot in range(4):
            values = turn(ends[0], -slot)
            for quarter in range(1, 4):
                values = jnp.where(group == quarter, turn(ends[quarter], quarter - slot), values)
            part, half = divmod(slot, 2)
            out_ref[part, half * HALF : (half + 1) * HALF, at : at + LANES] = values.astype(BF16)


def split(values):
    high = values.astype(BF16)
    return high, (values - high.astype(F32)).astype(BF16)


def turn_kernel(ritz_ref, turn_ref):
    real, imag = ritz_ref[0].T, ritz_ref[1].T
    for row, column, block in ((0, 0, real), (0, 1, -imag), (1, 0, imag), (1, 1, real)):
        turn_ref[row * MODES : (row + 1) * MODES, column * MODES : (column + 1) * MODES] = block.astype(BF16)


def split_kernel(ritz_ref, high_ref, low_ref):
    for part in range(2):
        high_ref[part], low_ref[part] = split(ritz_ref[part])


def left_kernel(ritz_ref, left_high_ref, left_low_ref):
    groups = (PEERS, 2, HALF, MODES)
    real, imag = ritz_ref[0].reshape(groups), ritz_ref[1].reshape(groups)
    for core in range(2):
        for part in range(2):
            one, two = (real, imag) if part == 0 else (-imag, real)
            values = jnp.concatenate([one[:, core], two[:, core]], axis=1).reshape(MODES, MODES).T
            rows = slice(part * MODES, (part + 1) * MODES)
            left_high_ref[core, rows, :], left_low_ref[core, rows, :] = split(values)


def rotate_kernel(got_ref, turn_ref, out_ref, stacked):
    packed = got_ref[:, TAIL_ROW:PIECE_ROWS, :].astype(F32)
    for part in range(2):
        rows = slice(part * MODES, (part + 1) * MODES)
        for block in range(2):
            at = (block * 2 + part) * OWNED
            stacked[rows, block * LANES : (block + 1) * LANES] = got_ref[:, at : at + OWNED, :].reshape(MODES, LANES)
        ends = jnp.concatenate([turn(packed, -2 * part), turn(packed, -2 * part - 1)], axis=1)
        stacked[rows, MAIN : MAIN + LANES] = ends.reshape(MODES, LANES).astype(BF16)

    owners = HALF_MODES // OWNED
    group = lane_group((owners, HALF, LANES))
    for step in range(2):
        peers = slice(step * owners, (step + 1) * owners)
        sent = None
        for part in range(2):
            at = part * MODES + step * HALF_MODES
            rotated = jnp.dot(turn_ref[at : at + HALF_MODES, :], stacked[...], preferred_element_type=F32)
            for block in range(2):
                row = (block * 2 + part) * OWNED
                values = rotated[:, block * LANES : (block + 1) * LANES].astype(BF16)
                out_ref[peers, row : row + OWNED, :] = values.reshape(owners, OWNED, LANES)
            ends = rotated[:, MAIN : MAIN + LANES].reshape(owners, OWNED, LANES)
            for half in range(2):
                moved = turn(ends[:, half * HALF : (half + 1) * HALF, :], part * 2 + half)
                sent = moved if sent is None else jnp.where(group == part * 2 + half, moved, sent)
        out_ref[peers, TAIL_ROW:PIECE_ROWS, :] = sent.astype(BF16)


def share_kernel(other, got_ref, out_ref, left, right):
    core = lax.rem(lax.axis_index("site"), 2)
    half = 1 - core if other else core
    group = lane_group((PEERS, HALF, LANES))

    def side(packed, row_half, sources, signs):
        first, second = (turn(packed, place - 2 * sources[place] - row_half) * signs[place] for place in range(2))
        return jnp.where(group == 0, first, jnp.where(group == 1, second, 0.0))

    packed = got_ref[:, TAIL_ROW:PIECE_ROWS, :].astype(F32)
    for part in range(2):
        for block in range(2):
            row = pl.multiple_of((block * 2 + part) * OWNED + half * HALF, HALF)
            at = part * MAIN + block * LANES
            left[:, at : at + LANES] = got_ref[:, pl.ds(row, HALF), :].reshape(HALF_MODES, LANES)
    ends = jnp.where(half == 0, side(packed, 0, (0, 1), (1, 1)), side(packed, 1, (0, 1), (1, 1)))
    left[:, 2 * MAIN : DEPTH] = ends.reshape(HALF_MODES, LANES).astype(BF16)

    packed = got_ref[:, PIECE_ROWS + TAIL_ROW : 2 * PIECE_ROWS, :].astype(F32)
    for part in range(2):
        sources, signs = ((0, 1), (1, 1)) if part == 0 else ((1, 0), (1, -1))
        for place in range(2):
            for block in range(2):
                at = PIECE_ROWS + (block * 2 + sources[place]) * OWNED
                values = got_ref[:, at : at + OWNED, :].reshape(MODES, LANES)
                lanes = slice(place * MAIN + block * LANES, place * MAIN + (block + 1) * LANES)
                right[part, :, lanes] = values if signs[place] > 0 else -values
        ends = jnp.concatenate([side(packed, row_half, sources, signs) for row_half in range(2)], axis=1)
        right[part, :, 2 * MAIN : DEPTH] = ends.reshape(MODES, LANES).astype(BF16)
    for part in range(2):
        share = lax.dot_general(left[...], right[part], NT, preferred_element_type=F32)
        for column in range(4):
            row = (part * 4 + column) * HALF
            values = share[:, column * LANES : (column + 1) * LANES].reshape(PEERS, HALF, LANES)
            out_ref[:, row : row + HALF, :] = values.astype(out_ref.dtype)


def assemble_kernel(kept_ref, taken_ref, turned_ref, out_ref):
    out_ref[:, 0:SHARE_ROWS, :] = (kept_ref[...] + taken_ref[...].astype(F32)).astype(BF16)
    out_ref[:, SHARE_ROWS:, :] = turned_ref[...]


def sum_kernel(back_ref, out_ref):
    total = back_ref[0, 0:SHARE_ROWS, :].astype(F32)
    for peer in range(1, PEERS):
        total += back_ref[peer, 0:SHARE_ROWS, :].astype(F32)
    total = total.astype(BF16)
    for part in range(2):
        for column in range(4):
            at = (part * 4 + column) * HALF
            for copy in range(out_ref.shape[0]):
                out_ref[copy, part * HALF : (part + 1) * HALF, column * LANES : (column + 1) * LANES] = total[
                    at : at + HALF, :
                ]


def total_of(pieces_ref):
    total = pieces_ref[0].astype(F32)
    for peer in range(1, pieces_ref.shape[0]):
        total += pieces_ref[peer].astype(F32)
    return total


def add_kernel(pieces_ref, out_ref):
    total = total_of(pieces_ref).astype(BF16)
    for copy in range(out_ref.shape[0]):
        out_ref[copy] = total


def project_kernel(pieces_ref, high_ref, low_ref, out_ref):
    high, low = split(total_of(pieces_ref))
    both = jnp.concatenate([high, low], axis=0)
    products = []
    for part in range(2):
        first = jnp.dot(both, high_ref[part], preferred_element_type=F32)
        second = jnp.dot(high, low_ref[part], preferred_element_type=F32)
        products.append(first[0:OWNED] + first[OWNED : 2 * OWNED] + second)
    real = products[0][0:HALF] - products[1][HALF:OWNED]
    imag = products[0][HALF:OWNED] + products[1][0:HALF]
    rows = jnp.concatenate([real, imag], axis=0).astype(BF16)
    for copy in range(out_ref.shape[0]):
        out_ref[copy] = rows


def finish_products(half, rows_ref, high_ref, low_ref, here):
    rows = rows_ref[...].reshape(MODES, MODES)
    total = jnp.dot(high_ref[half, here, :], rows, preferred_element_type=F32)
    return total + jnp.dot(low_ref[half, here, :], rows, preferred_element_type=F32)


def finish_own_kernel(rows_ref, high_ref, low_ref, out_ref):
    core = lax.rem(lax.axis_index("site"), 2)
    for part in range(2):
        out_ref[part] = finish_products(core, rows_ref, high_ref, low_ref, pl.ds(part * MODES, MODES))


def finish_other_kernel(rows_ref, high_ref, low_ref, first_ref, out_hbm, total, sent):
    core = lax.rem(lax.axis_index("site"), 2)
    copies = []
    for part in range(2):
        for half in range(2):
            rows = pl.ds(half * HALF_MODES, HALF_MODES)
            here = pl.ds(part * MODES + half * HALF_MODES, HALF_MODES)
            total[part, rows, :] = first_ref[part, rows, :] + finish_products(1 - core, rows_ref, high_ref, low_ref, here)
            copy = pltpu.make_async_copy(total.at[part, rows, :], out_hbm.at[part, rows, :], sent.at[part * 2 + half])
            copy.start()
            copies.append(copy)
    for copy in copies:
        copy.wait()


def call(kernel, name, outs, *args, flops=0, scratch=(), in_place=False, out_place=False, vmem=16):
    outs = tuple(jax.ShapeDtypeStruct(shape, dtype) for shape, dtype in outs)
    moved = sum(a.size * a.dtype.itemsize for a in args + outs)
    whole = pl.BlockSpec(memory_space=pltpu.VMEM)
    source = pl.BlockSpec(memory_space=pltpu.HBM) if in_place else whole
    target = pl.BlockSpec(memory_space=pltpu.HBM) if out_place else whole
    single = len(outs) == 1
    return pl.pallas_call(
        kernel,
        name=name,
        out_shape=outs[0] if single else outs,
        in_specs=[source] * len(args),
        out_specs=target if single else [target] * len(outs),
        scratch_shapes=list(scratch),
        cost_estimate=pl.CostEstimate(flops=flops, bytes_accessed=moved, transcendentals=0),
        compiler_params=pltpu.CompilerParams(vmem_limit_bytes=vmem * MIB),
    )(*args)


def exchange(pieces, axis, groups=None):
    return lax.all_to_all(pieces, axis, 0, 0, axis_index_groups=groups)


def on_device(site_count, vectors, images, ritz):
    cores, steps = range(2), range(NEAR)
    near_groups = [[[2 * (NEAR * h + z) + c for z in (3,2,1,0)] for h in steps] for c in cores]
    far_groups = [[[2 * (NEAR * h + z) + c for h in (2,1,3,0)] for z in steps] for c in cores]
    swap = [(i, i ^ 1) for i in range(site_count)]
    width = PEERS * MAIN + 4 * LANES
    share = (PEERS, SHARE_ROWS, LANES)
    square = (2 * MODES, 2 * MODES)
    local = [((2, OWNED, width), BF16)]

    packed = call(
        pack_kernel,
        "pack",
        [((PEERS, 2 * PIECE_ROWS, LANES), BF16)],
        vectors,
        images,
        scratch=[
            pltpu.VMEM((2, OWNED, width), BF16),
            pltpu.VMEM((2, OWNED, width), BF16),
            pltpu.VMEM((PEERS, 2 * PIECE_ROWS, LANES), BF16),
            pltpu.SemaphoreType.DMA((2 * CHUNKS + 2,)),
            pltpu.SemaphoreType.DMA((2 * CHUNKS + 2,)),
        ],
        in_place=True,
        out_place=True,
        vmem=60,
    )
    packed, ritz = lax.optimization_barrier((packed, ritz))
    factors = (
        call(turn_kernel, "turn_matrix", [(square, BF16)], ritz),
        call(left_kernel, "left_factors", [((2, 2 * MODES, MODES), BF16)] * 2, ritz),
        call(split_kernel, "split_ritz", [(ritz.shape, BF16)] * 2, ritz),
    )
    got, (turn_matrix, left, ritz_split) = lax.optimization_barrier((exchange(packed, "mode"), factors))

    sides = [pltpu.VMEM((HALF_MODES, DEPTH), BF16), pltpu.VMEM((2, MODES, DEPTH), BF16)]
    given = call(functools.partial(share_kernel, True), "share_given", [(share, BF16)], got, flops=10**9, scratch=sides)
    taken = lax.ppermute(given, "site", swap)
    kept = call(functools.partial(share_kernel, False), "share_kept", [(share, F32)], got, flops=10**9, scratch=sides)
    turned = call(
        rotate_kernel,
        "rotate",
        [((PEERS, PIECE_ROWS, LANES), BF16)],
        got,
        turn_matrix,
        flops=10**9,
        scratch=[pltpu.VMEM((2 * MODES, MAIN + LANES), BF16)],
    )
    sent = call(assemble_kernel, "assemble", [((PEERS, SHARE_ROWS + PIECE_ROWS, LANES), BF16)], kept, taken, turned)
    back = exchange(sent, "mode")
    summed = call(sum_kernel, "sum_shares", [((NEAR, OWNED, MODES), BF16)], back)
    summed = exchange(summed, "site", near_groups[0] + far_groups[1])
    summed = call(add_kernel, "add_shares", [((NEAR, OWNED, MODES), BF16)], summed)
    summed = exchange(summed, "site", far_groups[0] + near_groups[1])
    rows = call(project_kernel, "project", [((PEERS, OWNED, MODES), BF16)], summed, *ritz_split)
    own = exchange(rows, "mode")
    own, back = lax.optimization_barrier((own, back))
    other = lax.ppermute(own, "site", swap)
    rotated = call(unpack_kernel, "unpack", local, back)
    whole = [((2, MODES, MODES), F32)]
    first = call(finish_own_kernel, "finish_own", whole, own, *left, flops=10**9)
    projected = call(
        finish_other_kernel,
        "finish_other",
        whole,
        other,
        *left,
        first,
        flops=10**9,
        scratch=[pltpu.VMEM((2, MODES, MODES), F32), pltpu.SemaphoreType.DMA((4,))],
        out_place=True,
    )
    return rotated, projected


def solution(mesh):
    placed = (P(None, "mode", "site"), P(None, "mode", "site"), P())
    return jax.shard_map(
        functools.partial(on_device, mesh.shape["site"]),
        mesh=mesh,
        in_specs=placed,
        out_specs=(P(None, "mode", "site"), P()),
        check_vma=False,
    )
```

```python
import functools

import jax
import jax.numpy as jnp
from jax import lax
from jax.experimental import pallas as pl
from jax.experimental.pallas import tpu as pltpu
from jax.sharding import PartitionSpec as P

BF16 = jnp.bfloat16
F32 = jnp.float32
LANES = 128
MIB = 1024 * 1024

PEERS = 16
OWNED = 32
HALF = OWNED // 2
MODES = PEERS * OWNED
HALF_MODES = MODES // 2
MAIN = 2 * LANES
QUARTER = LANES // 4
TAIL_AT = PEERS * MAIN
TAIL_ROW = 4 * OWNED
PIECE_ROWS = TAIL_ROW + HALF
DEPTH = 2 * MAIN + LANES
SHARE_ROWS = 8 * HALF
CHUNKS = 2
NEAR = 4

REVERSED = list(range(PEERS))[::-1]

NT = (((1,), (1,)), ((), ()))


def lane_group(shape):
    return lax.broadcasted_iota(jnp.int32, shape, len(shape) - 1) // QUARTER


def turn(values, groups):
    shift = groups % 4 * QUARTER
    return pltpu.roll(values, shift, len(values.shape) - 1) if shift else values


def pack_kernel(vectors_hbm, images_hbm, out_hbm, vectors_ref, images_ref, out_ref, arrived, sent):
    peers = PEERS // CHUNKS
    copies = []
    for which, (source, target) in enumerate(((vectors_hbm, vectors_ref), (images_hbm, images_ref))):
        for chunk in range(CHUNKS + 1):
            at = chunk * peers * MAIN
            lanes = pl.ds(at, TAIL_AT // CHUNKS if chunk < CHUNKS else 4 * LANES)
            copy = pltpu.make_async_copy(
                source.at[:, :, lanes], target.at[:, :, lanes], arrived.at[which * (CHUNKS + 1) + chunk]
            )
            copy.start()
            copies.append(copy)
    group = lane_group((HALF, LANES))
    leaving = []
    for which, source_ref in enumerate((vectors_ref, images_ref)):
        base = which * PIECE_ROWS
        for chunk in range(CHUNKS + 1):
            index = which * (CHUNKS + 1) + chunk
            copies[index].wait()
            if chunk < CHUNKS:
                for peer in range(chunk * peers, (chunk + 1) * peers):
                    for block in range(2):
                        at = peer * MAIN + block * LANES
                        for part in range(2):
                            row = base + (block * 2 + part) * OWNED
                            out_ref[REVERSED[peer], row : row + OWNED, :] = source_ref[part, :, at : at + LANES]
                where = (pl.ds(PEERS - (chunk + 1) * peers, peers), pl.ds(base, TAIL_ROW))
            else:
                for block in range(PEERS // 4):
                    at = TAIL_AT + block * LANES
                    tails = [
                        source_ref[part, half * HALF : (half + 1) * HALF, at : at + LANES].astype(F32)
                        for part in range(2)
                        for half in range(2)
                    ]
                    for quarter in range(4):
                        packed = turn(tails[0], -quarter)
                        for slot in range(1, 4):
                            packed = jnp.where(group == slot, turn(tails[slot], slot - quarter), packed)
                        out_ref[REVERSED[block * 4 + quarter], base + TAIL_ROW : base + PIECE_ROWS, :] = packed.astype(BF16)
                where = (pl.ds(0, PEERS), pl.ds(base + TAIL_ROW, HALF))
            copy = pltpu.make_async_copy(out_ref.at[where], out_hbm.at[where], sent.at[index])
            copy.start()
            leaving.append(copy)
    for copy in leaving:
        copy.wait()


def of_owners(got_ref, rows):
    return jnp.concatenate([got_ref[at, rows, :] for at in REVERSED], axis=0)


def tails_of(got_ref, base):
    values = of_owners(got_ref, slice(base + TAIL_ROW, base + PIECE_ROWS)).astype(F32)
    return values.reshape(PEERS, HALF, LANES)


def unpack_kernel(back_ref, out_ref):
    for peer in range(PEERS):
        for block in range(2):
            at = peer * MAIN + block * LANES
            for part in range(2):
                row = SHARE_ROWS + (block * 2 + part) * OWNED
                out_ref[part, :, at : at + LANES] = back_ref[REVERSED[peer], row : row + OWNED, :]
    group = lane_group((HALF, LANES))
    for block in range(PEERS // 4):
        ends = [back_ref[REVERSED[block * 4 + quarter], SHARE_ROWS + TAIL_ROW : SHARE_ROWS + PIECE_ROWS, :].astype(F32) for quarter in range(4)]
        at = TAIL_AT + block * LANES
        for slot in range(4):
            values = turn(ends[0], -slot)
            for quarter in range(1, 4):
                values = jnp.where(group == quarter, turn(ends[quarter], quarter - slot), values)
            part, half = divmod(slot, 2)
            out_ref[part, half * HALF : (half + 1) * HALF, at : at + LANES] = values.astype(BF16)


def split(values):
    high = values.astype(BF16)
    return high, (values - high.astype(F32)).astype(BF16)


def turn_kernel(ritz_ref, turn_ref):
    real, imag = ritz_ref[0].T, ritz_ref[1].T
    for row, column, block in ((0, 0, real), (0, 1, -imag), (1, 0, imag), (1, 1, real)):
        turn_ref[row * MODES : (row + 1) * MODES, column * MODES : (column + 1) * MODES] = block.astype(BF16)


def split_kernel(ritz_ref, high_ref, low_ref):
    for part in range(2):
        high_ref[part], low_ref[part] = split(ritz_ref[part])


def left_kernel(ritz_ref, left_high_ref, left_low_ref):
    groups = (PEERS, 2, HALF, MODES)
    real, imag = ritz_ref[0].reshape(groups), ritz_ref[1].reshape(groups)
    for core in range(2):
        for part in range(2):
            one, two = (real, imag) if part == 0 else (-imag, real)
            values = jnp.concatenate([side[owner, core] for owner in REVERSED for side in (one, two)], axis=0).T
            rows = slice(part * MODES, (part + 1) * MODES)
            left_high_ref[core, rows, :], left_low_ref[core, rows, :] = split(values)


def rotate_kernel(got_ref, turn_ref, out_ref, stacked):
    packed = tails_of(got_ref, 0)
    for part in range(2):
        rows = slice(part * MODES, (part + 1) * MODES)
        for block in range(2):
            at = (block * 2 + part) * OWNED
            stacked[rows, block * LANES : (block + 1) * LANES] = of_owners(got_ref, slice(at, at + OWNED))
        ends = jnp.concatenate([turn(packed, -2 * part), turn(packed, -2 * part - 1)], axis=1)
        stacked[rows, MAIN : MAIN + LANES] = ends.reshape(MODES, LANES).astype(BF16)

    owners = HALF_MODES // OWNED
    group = lane_group((owners, HALF, LANES))
    for step in range(2):
        places = REVERSED[step * owners : (step + 1) * owners]
        sent = None
        for part in range(2):
            at = part * MODES + step * HALF_MODES
            rotated = jnp.dot(turn_ref[at : at + HALF_MODES, :], stacked[...], preferred_element_type=F32)
            for block in range(2):
                row = (block * 2 + part) * OWNED
                values = rotated[:, block * LANES : (block + 1) * LANES].astype(BF16)
                for owner, place in enumerate(places):
                    out_ref[place, row : row + OWNED, :] = values[owner * OWNED : (owner + 1) * OWNED, :]
            ends = rotated[:, MAIN : MAIN + LANES].reshape(owners, OWNED, LANES)
            for half in range(2):
                moved = turn(ends[:, half * HALF : (half + 1) * HALF, :], part * 2 + half)
                sent = moved if sent is None else jnp.where(group == part * 2 + half, moved, sent)
        for owner, place in enumerate(places):
            out_ref[place, TAIL_ROW:PIECE_ROWS, :] = sent[owner].astype(BF16)


def share_kernel(other, got_ref, out_ref, left, right):
    core = lax.rem(lax.axis_index("site"), 2)
    half = 1 - core if other else core
    group = lane_group((PEERS, HALF, LANES))

    def side(packed, row_half, sources, signs):
        first, second = (turn(packed, place - 2 * sources[place] - row_half) * signs[place] for place in range(2))
        return jnp.where(group == 0, first, jnp.where(group == 1, second, 0.0))

    packed = got_ref[:, TAIL_ROW:PIECE_ROWS, :].astype(F32)
    for part in range(2):
        for block in range(2):
            row = pl.multiple_of((block * 2 + part) * OWNED + half * HALF, HALF)
            at = part * MAIN + block * LANES
            left[:, at : at + LANES] = got_ref[:, pl.ds(row, HALF), :].reshape(HALF_MODES, LANES)
    ends = jnp.where(half == 0, side(packed, 0, (0, 1), (1, 1)), side(packed, 1, (0, 1), (1, 1)))
    left[:, 2 * MAIN : DEPTH] = ends.reshape(HALF_MODES, LANES).astype(BF16)

    packed = tails_of(got_ref, PIECE_ROWS)
    for part in range(2):
        sources, signs = ((0, 1), (1, 1)) if part == 0 else ((1, 0), (1, -1))
        for place in range(2):
            for block in range(2):
                at = PIECE_ROWS + (block * 2 + sources[place]) * OWNED
                values = of_owners(got_ref, slice(at, at + OWNED))
                lanes = slice(place * MAIN + block * LANES, place * MAIN + (block + 1) * LANES)
                right[part, :, lanes] = values if signs[place] > 0 else -values
        ends = jnp.concatenate([side(packed, row_half, sources, signs) for row_half in range(2)], axis=1)
        right[part, :, 2 * MAIN : DEPTH] = ends.reshape(MODES, LANES).astype(BF16)
    for part in range(2):
        share = lax.dot_general(left[...], right[part], NT, preferred_element_type=F32)
        for column in range(4):
            row = (part * 4 + column) * HALF
            values = share[:, column * LANES : (column + 1) * LANES].reshape(PEERS, HALF, LANES)
            out_ref[:, row : row + HALF, :] = values.astype(out_ref.dtype)


def assemble_kernel(kept_ref, taken_ref, turned_ref, out_ref):
    out_ref[:, 0:SHARE_ROWS, :] = (kept_ref[...] + taken_ref[...].astype(F32)).astype(BF16)
    out_ref[:, SHARE_ROWS:, :] = turned_ref[...]


def sum_kernel(back_ref, out_ref):
    total = back_ref[0, 0:SHARE_ROWS, :].astype(F32)
    for peer in range(1, PEERS):
        total += back_ref[peer, 0:SHARE_ROWS, :].astype(F32)
    total = total.astype(BF16)
    for part in range(2):
        for column in range(4):
            at = (part * 4 + column) * HALF
            for copy in range(out_ref.shape[0]):
                out_ref[copy, part * HALF : (part + 1) * HALF, column * LANES : (column + 1) * LANES] = total[
                    at : at + HALF, :
                ]


def total_of(pieces_ref):
    total = pieces_ref[0].astype(F32)
    for peer in range(1, pieces_ref.shape[0]):
        total += pieces_ref[peer].astype(F32)
    return total


def add_kernel(pieces_ref, out_ref):
    total = total_of(pieces_ref).astype(BF16)
    for copy in range(out_ref.shape[0]):
        out_ref[copy] = total


def project_kernel(pieces_ref, high_ref, low_ref, out_ref):
    high, low = split(total_of(pieces_ref))
    both = jnp.concatenate([high, low], axis=0)
    products = []
    for part in range(2):
        first = jnp.dot(both, high_ref[part], preferred_element_type=F32)
        second = jnp.dot(high, low_ref[part], preferred_element_type=F32)
        products.append(first[0:OWNED] + first[OWNED : 2 * OWNED] + second)
    real = products[0][0:HALF] - products[1][HALF:OWNED]
    imag = products[0][HALF:OWNED] + products[1][0:HALF]
    rows = jnp.concatenate([real, imag], axis=0).astype(BF16)
    for copy in range(out_ref.shape[0]):
        out_ref[copy] = rows


def finish_products(half, rows_ref, high_ref, low_ref, here):
    rows = rows_ref[...].reshape(MODES, MODES)
    total = jnp.dot(high_ref[half, here, :], rows, preferred_element_type=F32)
    return total + jnp.dot(low_ref[half, here, :], rows, preferred_element_type=F32)


def finish_own_kernel(rows_ref, high_ref, low_ref, out_ref):
    core = lax.rem(lax.axis_index("site"), 2)
    for part in range(2):
        out_ref[part] = finish_products(core, rows_ref, high_ref, low_ref, pl.ds(part * MODES, MODES))


def finish_other_kernel(rows_ref, high_ref, low_ref, first_ref, out_hbm, total, sent):
    core = lax.rem(lax.axis_index("site"), 2)
    copies = []
    for part in range(2):
        for half in range(2):
            rows = pl.ds(half * HALF_MODES, HALF_MODES)
            here = pl.ds(part * MODES + half * HALF_MODES, HALF_MODES)
            total[part, rows, :] = first_ref[part, rows, :] + finish_products(1 - core, rows_ref, high_ref, low_ref, here)
            copy = pltpu.make_async_copy(total.at[part, rows, :], out_hbm.at[part, rows, :], sent.at[part * 2 + half])
            copy.start()
            copies.append(copy)
    for copy in copies:
        copy.wait()


def call(kernel, name, outs, *args, flops=0, scratch=(), in_place=False, out_place=False, vmem=16):
    outs = tuple(jax.ShapeDtypeStruct(shape, dtype) for shape, dtype in outs)
    moved = sum(a.size * a.dtype.itemsize for a in args + outs)
    whole = pl.BlockSpec(memory_space=pltpu.VMEM)
    source = pl.BlockSpec(memory_space=pltpu.HBM) if in_place else whole
    target = pl.BlockSpec(memory_space=pltpu.HBM) if out_place else whole
    single = len(outs) == 1
    return pl.pallas_call(
        kernel,
        name=name,
        out_shape=outs[0] if single else outs,
        in_specs=[source] * len(args),
        out_specs=target if single else [target] * len(outs),
        scratch_shapes=list(scratch),
        cost_estimate=pl.CostEstimate(flops=flops, bytes_accessed=moved, transcendentals=0),
        compiler_params=pltpu.CompilerParams(vmem_limit_bytes=vmem * MIB),
    )(*args)


def exchange(pieces, axis, groups=None):
    return lax.all_to_all(pieces, axis, 0, 0, axis_index_groups=groups)


def on_device(site_count, vectors, images, ritz):
    cores, steps = range(2), range(NEAR)
    near_groups = [[[2 * (NEAR * h + z) + c for z in (3,2,1,0)] for h in steps] for c in cores]
    far_groups = [[[2 * (NEAR * h + z) + c for h in (2,1,3,0)] for z in steps] for c in cores]
    swap = [(i, i ^ 1) for i in range(site_count)]
    width = PEERS * MAIN + 4 * LANES
    share = (PEERS, SHARE_ROWS, LANES)
    square = (2 * MODES, 2 * MODES)
    local = [((2, OWNED, width), BF16)]

    packed = call(
        pack_kernel,
        "pack",
        [((PEERS, 2 * PIECE_ROWS, LANES), BF16)],
        vectors,
        images,
        scratch=[
            pltpu.VMEM((2, OWNED, width), BF16),
            pltpu.VMEM((2, OWNED, width), BF16),
            pltpu.VMEM((PEERS, 2 * PIECE_ROWS, LANES), BF16),
            pltpu.SemaphoreType.DMA((2 * CHUNKS + 2,)),
            pltpu.SemaphoreType.DMA((2 * CHUNKS + 2,)),
        ],
        in_place=True,
        out_place=True,
        vmem=60,
    )
    packed, ritz = lax.optimization_barrier((packed, ritz))
    factors = (
        call(turn_kernel, "turn_matrix", [(square, BF16)], ritz),
        call(left_kernel, "left_factors", [((2, 2 * MODES, MODES), BF16)] * 2, ritz),
        call(split_kernel, "split_ritz", [(ritz.shape, BF16)] * 2, ritz),
    )
    got, (turn_matrix, left, ritz_split) = lax.optimization_barrier((exchange(packed, "mode", [REVERSED]), factors))

    sides = [pltpu.VMEM((HALF_MODES, DEPTH), BF16), pltpu.VMEM((2, MODES, DEPTH), BF16)]
    given = call(functools.partial(share_kernel, True), "share_given", [(share, BF16)], got, flops=10**9, scratch=sides)
    taken = lax.ppermute(given, "site", swap)
    kept = call(functools.partial(share_kernel, False), "share_kept", [(share, F32)], got, flops=10**9, scratch=sides)
    turned = call(
        rotate_kernel,
        "rotate",
        [((PEERS, PIECE_ROWS, LANES), BF16)],
        got,
        turn_matrix,
        flops=10**9,
        scratch=[pltpu.VMEM((2 * MODES, MAIN + LANES), BF16)],
    )
    sent = call(assemble_kernel, "assemble", [((PEERS, SHARE_ROWS + PIECE_ROWS, LANES), BF16)], kept, taken, turned)
    back = exchange(sent, "mode", [REVERSED])
    summed = call(sum_kernel, "sum_shares", [((NEAR, OWNED, MODES), BF16)], back)
    summed = exchange(summed, "site", near_groups[0] + far_groups[1])
    summed = call(add_kernel, "add_shares", [((NEAR, OWNED, MODES), BF16)], summed)
    summed = exchange(summed, "site", far_groups[0] + near_groups[1])
    rows = call(project_kernel, "project", [((PEERS, OWNED, MODES), BF16)], summed, *ritz_split)
    own = exchange(rows, "mode", [REVERSED])
    own, back = lax.optimization_barrier((own, back))
    other = lax.ppermute(own, "site", swap)
    rotated = call(unpack_kernel, "unpack", local, back)
    whole = [((2, MODES, MODES), F32)]
    first = call(finish_own_kernel, "finish_own", whole, own, *left, flops=10**9)
    projected = call(
        finish_other_kernel,
        "finish_other",
        whole,
        other,
        *left,
        first,
        flops=10**9,
        scratch=[pltpu.VMEM((2, MODES, MODES), F32), pltpu.SemaphoreType.DMA((4,))],
        out_place=True,
    )
    return rotated, projected


def solution(mesh):
    placed = (P(None, "mode", "site"), P(None, "mode", "site"), P())
    return jax.shard_map(
        functools.partial(on_device, mesh.shape["site"]),
        mesh=mesh,
        in_specs=placed,
        out_specs=(P(None, "mode", "site"), P()),
        check_vma=False,
    )
```

```python
import functools

import jax
import jax.numpy as jnp
from jax import lax
from jax.experimental import pallas as pl
from jax.experimental.pallas import tpu as pltpu
from jax.sharding import PartitionSpec as P

BF16 = jnp.bfloat16
F32 = jnp.float32
LANES = 128
MIB = 1024 * 1024

PEERS = 16
OWNED = 32
HALF = OWNED // 2
MODES = PEERS * OWNED
HALF_MODES = MODES // 2
MAIN = 2 * LANES
QUARTER = LANES // 4
TAIL_AT = PEERS * MAIN
TAIL_ROW = 4 * OWNED
PIECE_ROWS = TAIL_ROW + HALF
DEPTH = 2 * MAIN + LANES
SHARE_ROWS = 8 * HALF
CHUNKS = 4
NEAR = 4

REVERSED = list(range(PEERS))[::-1]

NT = (((1,), (1,)), ((), ()))


def lane_group(shape):
    return lax.broadcasted_iota(jnp.int32, shape, len(shape) - 1) // QUARTER


def turn(values, groups):
    shift = groups % 4 * QUARTER
    return pltpu.roll(values, shift, len(values.shape) - 1) if shift else values


def pack_kernel(vectors_hbm, images_hbm, out_hbm, sources_ref, out_ref, arrived, sent):
    peers = PEERS // CHUNKS
    copies, leaving = {}, []
    for chunk in (CHUNKS, *range(CHUNKS)):
        for which, source in enumerate((vectors_hbm, images_hbm)):
            lanes = pl.ds(chunk * peers * MAIN, peers * MAIN if chunk < CHUNKS else 4 * LANES)
            copies[which, chunk] = pltpu.make_async_copy(
                source.at[:, :, lanes], sources_ref.at[which, :, :, lanes], arrived.at[which * (CHUNKS + 1) + chunk]
            )
            copies[which, chunk].start()
    group = lane_group((HALF, LANES))
    for which in range(2):
        copies[which, CHUNKS].wait()
        for block in range(PEERS // 4):
            at = slice(TAIL_AT + block * LANES, TAIL_AT + (block + 1) * LANES)
            tails = [
                sources_ref[which, part, half * HALF : (half + 1) * HALF, at].astype(F32)
                for part in range(2)
                for half in range(2)
            ]
            for quarter in range(4):
                packed = turn(tails[0], -quarter)
                for slot in range(1, 4):
                    packed = jnp.where(group == slot, turn(tails[slot], slot - quarter), packed)
                place, lanes = REVERSED[block * 4 + quarter], slice(which * LANES, (which + 1) * LANES)
                out_ref[place, 4 * OWNED : 4 * OWNED + HALF, lanes] = packed.astype(BF16)
    for chunk in range(CHUNKS):
        for which in range(2):
            copies[which, chunk].wait()
            for peer in range(chunk * peers, (chunk + 1) * peers):
                for part in range(2):
                    row = (which * 2 + part) * OWNED
                    out_ref[REVERSED[peer], row : row + OWNED, :] = sources_ref[
                        which, part, :, peer * MAIN : (peer + 1) * MAIN
                    ]
        places = pl.ds(PEERS - (chunk + 1) * peers, peers)
        copy = pltpu.make_async_copy(out_ref.at[places], out_hbm.at[places], sent.at[chunk])
        copy.start()
        leaving.append(copy)
    for copy in leaving:
        copy.wait()


def main_of(got_ref, which, part):
    at = (which * 2 + part) * OWNED
    return jnp.concatenate([got_ref[place, at : at + OWNED, :] for place in REVERSED], axis=0)


def tails_of(got_ref, which, places):
    lanes = slice(which * LANES, (which + 1) * LANES)
    values = [got_ref[place, 4 * OWNED : 4 * OWNED + HALF, lanes] for place in places]
    return jnp.concatenate(values, axis=0).astype(F32).reshape(PEERS, HALF, LANES)


def unpack_kernel(back_ref, out_ref):
    for peer in range(PEERS):
        for block in range(2):
            at = peer * MAIN + block * LANES
            for part in range(2):
                row = SHARE_ROWS + (block * 2 + part) * OWNED
                out_ref[part, :, at : at + LANES] = back_ref[REVERSED[peer], row : row + OWNED, :]
    group = lane_group((HALF, LANES))
    for block in range(PEERS // 4):
        ends = [back_ref[REVERSED[block * 4 + quarter], SHARE_ROWS + TAIL_ROW : SHARE_ROWS + PIECE_ROWS, :].astype(F32) for quarter in range(4)]
        at = TAIL_AT + block * LANES
        for slot in range(4):
            values = turn(ends[0], -slot)
            for quarter in range(1, 4):
                values = jnp.where(group == quarter, turn(ends[quarter], quarter - slot), values)
            part, half = divmod(slot, 2)
            out_ref[part, half * HALF : (half + 1) * HALF, at : at + LANES] = values.astype(BF16)


def split(values):
    high = values.astype(BF16)
    return high, (values - high.astype(F32)).astype(BF16)


def turn_kernel(ritz_ref, turn_ref):
    real, imag = ritz_ref[0].T, ritz_ref[1].T
    for row, column, block in ((0, 0, real), (0, 1, -imag), (1, 0, imag), (1, 1, real)):
        turn_ref[row * MODES : (row + 1) * MODES, column * MODES : (column + 1) * MODES] = block.astype(BF16)


def split_kernel(ritz_ref, high_ref, low_ref):
    for part in range(2):
        high_ref[part], low_ref[part] = split(ritz_ref[part])


def left_kernel(ritz_ref, left_high_ref, left_low_ref):
    groups = (PEERS, 2, HALF, MODES)
    real, imag = ritz_ref[0].reshape(groups), ritz_ref[1].reshape(groups)
    for core in range(2):
        for part in range(2):
            one, two = (real, imag) if part == 0 else (-imag, real)
            values = jnp.concatenate([side[owner, core] for owner in REVERSED for side in (one, two)], axis=0).T
            rows = slice(part * MODES, (part + 1) * MODES)
            left_high_ref[core, rows, :], left_low_ref[core, rows, :] = split(values)


def rotate_kernel(got_ref, turn_ref, out_ref, stacked):
    packed = tails_of(got_ref, 0, REVERSED)
    for part in range(2):
        rows = slice(part * MODES, (part + 1) * MODES)
        stacked[rows, 0:MAIN] = main_of(got_ref, 0, part)
        ends = jnp.concatenate([turn(packed, -2 * part), turn(packed, -2 * part - 1)], axis=1)
        stacked[rows, MAIN : MAIN + LANES] = ends.reshape(MODES, LANES).astype(BF16)

    owners = HALF_MODES // OWNED
    group = lane_group((owners, HALF, LANES))
    for step in range(2):
        places = REVERSED[step * owners : (step + 1) * owners]
        sent = None
        for part in range(2):
            at = part * MODES + step * HALF_MODES
            rotated = jnp.dot(turn_ref[at : at + HALF_MODES, :], stacked[...], preferred_element_type=F32)
            for block in range(2):
                row = (block * 2 + part) * OWNED
                values = rotated[:, block * LANES : (block + 1) * LANES].astype(BF16)
                for owner, place in enumerate(places):
                    out_ref[place, row : row + OWNED, :] = values[owner * OWNED : (owner + 1) * OWNED, :]
            ends = rotated[:, MAIN : MAIN + LANES].reshape(owners, OWNED, LANES)
            for half in range(2):
                moved = turn(ends[:, half * HALF : (half + 1) * HALF, :], part * 2 + half)
                sent = moved if sent is None else jnp.where(group == part * 2 + half, moved, sent)
        for owner, place in enumerate(places):
            out_ref[place, TAIL_ROW:PIECE_ROWS, :] = sent[owner].astype(BF16)


def share_kernel(other, got_ref, out_ref, left, right):
    core = lax.rem(lax.axis_index("site"), 2)
    half = 1 - core if other else core
    group = lane_group((PEERS, HALF, LANES))

    def side(packed, row_half, sources, signs):
        first, second = (turn(packed, place - 2 * sources[place] - row_half) * signs[place] for place in range(2))
        return jnp.where(group == 0, first, jnp.where(group == 1, second, 0.0))

    packed = tails_of(got_ref, 0, range(PEERS))
    for part in range(2):
        row = pl.multiple_of(part * OWNED + half * HALF, HALF)
        left[:, part * MAIN : (part + 1) * MAIN] = got_ref[:, pl.ds(row, HALF), :].reshape(HALF_MODES, MAIN)
    ends = jnp.where(half == 0, side(packed, 0, (0, 1), (1, 1)), side(packed, 1, (0, 1), (1, 1)))
    left[:, 2 * MAIN : DEPTH] = ends.reshape(HALF_MODES, LANES).astype(BF16)

    packed = tails_of(got_ref, 1, REVERSED)
    for part in range(2):
        sources, signs = ((0, 1), (1, 1)) if part == 0 else ((1, 0), (1, -1))
        for place in range(2):
            values = main_of(got_ref, 1, sources[place])
            right[part, :, place * MAIN : (place + 1) * MAIN] = values if signs[place] > 0 else -values
        ends = jnp.concatenate([side(packed, row_half, sources, signs) for row_half in range(2)], axis=1)
        right[part, :, 2 * MAIN : DEPTH] = ends.reshape(MODES, LANES).astype(BF16)
    for part in range(2):
        share = lax.dot_general(left[...], right[part], NT, preferred_element_type=F32)
        for column in range(4):
            row = (part * 4 + column) * HALF
            values = share[:, column * LANES : (column + 1) * LANES].reshape(PEERS, HALF, LANES)
            out_ref[:, row : row + HALF, :] = values.astype(out_ref.dtype)


def assemble_kernel(kept_ref, taken_ref, turned_ref, out_ref):
    out_ref[:, 0:SHARE_ROWS, :] = (kept_ref[...] + taken_ref[...].astype(F32)).astype(BF16)
    out_ref[:, SHARE_ROWS:, :] = turned_ref[...]


def sum_kernel(back_ref, out_ref):
    total = back_ref[0, 0:SHARE_ROWS, :].astype(F32)
    for peer in range(1, PEERS):
        total += back_ref[peer, 0:SHARE_ROWS, :].astype(F32)
    total = total.astype(BF16)
    for part in range(2):
        for column in range(4):
            at = (part * 4 + column) * HALF
            for copy in range(out_ref.shape[0]):
                out_ref[copy, part * HALF : (part + 1) * HALF, column * LANES : (column + 1) * LANES] = total[
                    at : at + HALF, :
                ]


def total_of(pieces_ref):
    total = pieces_ref[0].astype(F32)
    for peer in range(1, pieces_ref.shape[0]):
        total += pieces_ref[peer].astype(F32)
    return total


def add_kernel(pieces_ref, out_ref):
    total = total_of(pieces_ref).astype(BF16)
    for copy in range(out_ref.shape[0]):
        out_ref[copy] = total


def project_kernel(pieces_ref, high_ref, low_ref, out_ref):
    high, low = split(total_of(pieces_ref))
    both = jnp.concatenate([high, low], axis=0)
    products = []
    for part in range(2):
        first = jnp.dot(both, high_ref[part], preferred_element_type=F32)
        second = jnp.dot(high, low_ref[part], preferred_element_type=F32)
        products.append(first[0:OWNED] + first[OWNED : 2 * OWNED] + second)
    real = products[0][0:HALF] - products[1][HALF:OWNED]
    imag = products[0][HALF:OWNED] + products[1][0:HALF]
    rows = jnp.concatenate([real, imag], axis=0).astype(BF16)
    for copy in range(out_ref.shape[0]):
        out_ref[copy] = rows


def finish_products(half, rows_ref, high_ref, low_ref, here):
    rows = rows_ref[...].reshape(MODES, MODES)
    total = jnp.dot(high_ref[half, here, :], rows, preferred_element_type=F32)
    return total + jnp.dot(low_ref[half, here, :], rows, preferred_element_type=F32)


def finish_own_kernel(rows_ref, high_ref, low_ref, out_ref):
    core = lax.rem(lax.axis_index("site"), 2)
    for part in range(2):
        out_ref[part] = finish_products(core, rows_ref, high_ref, low_ref, pl.ds(part * MODES, MODES))


def finish_other_kernel(rows_ref, high_ref, low_ref, first_ref, out_hbm, total, sent):
    core = lax.rem(lax.axis_index("site"), 2)
    copies = []
    for part in range(2):
        for half in range(2):
            rows = pl.ds(half * HALF_MODES, HALF_MODES)
            here = pl.ds(part * MODES + half * HALF_MODES, HALF_MODES)
            total[part, rows, :] = first_ref[part, rows, :] + finish_products(1 - core, rows_ref, high_ref, low_ref, here)
            copy = pltpu.make_async_copy(total.at[part, rows, :], out_hbm.at[part, rows, :], sent.at[part * 2 + half])
            copy.start()
            copies.append(copy)
    for copy in copies:
        copy.wait()


def call(kernel, name, outs, *args, flops=0, scratch=(), in_place=False, out_place=False, vmem=16):
    outs = tuple(jax.ShapeDtypeStruct(shape, dtype) for shape, dtype in outs)
    moved = sum(a.size * a.dtype.itemsize for a in args + outs)
    whole = pl.BlockSpec(memory_space=pltpu.VMEM)
    source = pl.BlockSpec(memory_space=pltpu.HBM) if in_place else whole
    target = pl.BlockSpec(memory_space=pltpu.HBM) if out_place else whole
    single = len(outs) == 1
    return pl.pallas_call(
        kernel,
        name=name,
        out_shape=outs[0] if single else outs,
        in_specs=[source] * len(args),
        out_specs=target if single else [target] * len(outs),
        scratch_shapes=list(scratch),
        cost_estimate=pl.CostEstimate(flops=flops, bytes_accessed=moved, transcendentals=0),
        compiler_params=pltpu.CompilerParams(vmem_limit_bytes=vmem * MIB),
    )(*args)


def exchange(pieces, axis, groups=None):
    return lax.all_to_all(pieces, axis, 0, 0, axis_index_groups=groups)


def on_device(site_count, vectors, images, ritz):
    cores, steps = range(2), range(NEAR)
    near_groups = [[[2 * (NEAR * h + z) + c for z in (3,2,1,0)] for h in steps] for c in cores]
    far_groups = [[[2 * (NEAR * h + z) + c for h in (2,1,3,0)] for z in steps] for c in cores]
    swap = [(i, i ^ 1) for i in range(site_count)]
    width = PEERS * MAIN + 4 * LANES
    share = (PEERS, SHARE_ROWS, LANES)
    square = (2 * MODES, 2 * MODES)
    local = [((2, OWNED, width), BF16)]

    packed = call(
        pack_kernel,
        "pack",
        [((PEERS, 4 * OWNED + HALF, MAIN), BF16)],
        vectors,
        images,
        scratch=[
            pltpu.VMEM((2, 2, OWNED, width), BF16),
            pltpu.VMEM((PEERS, 4 * OWNED + HALF, MAIN), BF16),
            pltpu.SemaphoreType.DMA((2 * CHUNKS + 2,)),
            pltpu.SemaphoreType.DMA((CHUNKS,)),
        ],
        in_place=True,
        out_place=True,
        vmem=60,
    )
    packed, ritz = lax.optimization_barrier((packed, ritz))
    factors = (
        call(turn_kernel, "turn_matrix", [(square, BF16)], ritz),
        call(left_kernel, "left_factors", [((2, 2 * MODES, MODES), BF16)] * 2, ritz),
        call(split_kernel, "split_ritz", [(ritz.shape, BF16)] * 2, ritz),
    )
    got, (turn_matrix, left, ritz_split) = lax.optimization_barrier((exchange(packed, "mode", [REVERSED]), factors))

    sides = [pltpu.VMEM((HALF_MODES, DEPTH), BF16), pltpu.VMEM((2, MODES, DEPTH), BF16)]
    given = call(functools.partial(share_kernel, True), "share_given", [(share, BF16)], got, flops=10**9, scratch=sides)
    taken = lax.ppermute(given, "site", swap)
    kept = call(functools.partial(share_kernel, False), "share_kept", [(share, F32)], got, flops=10**9, scratch=sides)
    turned = call(
        rotate_kernel,
        "rotate",
        [((PEERS, PIECE_ROWS, LANES), BF16)],
        got,
        turn_matrix,
        flops=10**9,
        scratch=[pltpu.VMEM((2 * MODES, MAIN + LANES), BF16)],
    )
    sent = call(assemble_kernel, "assemble", [((PEERS, SHARE_ROWS + PIECE_ROWS, LANES), BF16)], kept, taken, turned)
    back = exchange(sent, "mode", [REVERSED])
    summed = call(sum_kernel, "sum_shares", [((NEAR, OWNED, MODES), BF16)], back)
    summed = exchange(summed, "site", far_groups[0] + near_groups[1])
    summed = call(add_kernel, "add_shares", [((NEAR, OWNED, MODES), BF16)], summed)
    summed = exchange(summed, "site", near_groups[0] + far_groups[1])
    rows = call(project_kernel, "project", [((PEERS, OWNED, MODES), BF16)], summed, *ritz_split)
    own = exchange(rows, "mode", [REVERSED])
    own, back = lax.optimization_barrier((own, back))
    other = lax.ppermute(own, "site", swap)
    rotated = call(unpack_kernel, "unpack", local, back)
    whole = [((2, MODES, MODES), F32)]
    first = call(finish_own_kernel, "finish_own", whole, own, *left, flops=10**9)
    projected = call(
        finish_other_kernel,
        "finish_other",
        whole,
        other,
        *left,
        first,
        flops=10**9,
        scratch=[pltpu.VMEM((2, MODES, MODES), F32), pltpu.SemaphoreType.DMA((4,))],
        out_place=True,
    )
    return rotated, projected


def solution(mesh):
    placed = (P(None, "mode", "site"), P(None, "mode", "site"), P())
    return jax.shard_map(
        functools.partial(on_device, mesh.shape["site"]),
        mesh=mesh,
        in_specs=placed,
        out_specs=(P(None, "mode", "site"), P()),
        check_vma=False,
    )
```

```python
import functools

import jax
import jax.numpy as jnp
from jax import lax
from jax.experimental import pallas as pl
from jax.experimental.pallas import tpu as pltpu
from jax.sharding import PartitionSpec as P

BF16 = jnp.bfloat16
F32 = jnp.float32
LANES = 128
MIB = 1024 * 1024

PEERS = 16
OWNED = 32
HALF = OWNED // 2
MODES = PEERS * OWNED
HALF_MODES = MODES // 2
MAIN = 2 * LANES
QUARTER = LANES // 4
TAIL_AT = PEERS * MAIN
TAIL_ROW = 4 * OWNED
PIECE_ROWS = TAIL_ROW + HALF
DEPTH = 2 * MAIN + LANES
SHARE_ROWS = 8 * HALF
CHUNKS = 4
NEAR = 4

REVERSED = list(range(PEERS))[::-1]

NT = (((1,), (1,)), ((), ()))


def lane_group(shape):
    return lax.broadcasted_iota(jnp.int32, shape, len(shape) - 1) // QUARTER


def turn(values, groups):
    shift = groups % 4 * QUARTER
    return pltpu.roll(values, shift, len(values.shape) - 1) if shift else values


def pack_kernel(vectors_hbm, images_hbm, out_hbm, sources_ref, out_ref, arrived, sent):
    peers = PEERS // CHUNKS
    copies, leaving = {}, []
    for chunk in (CHUNKS, *range(CHUNKS)):
        for which, source in enumerate((vectors_hbm, images_hbm)):
            lanes = pl.ds(chunk * peers * MAIN, peers * MAIN if chunk < CHUNKS else 4 * LANES)
            copies[which, chunk] = pltpu.make_async_copy(
                source.at[:, :, lanes], sources_ref.at[which, :, :, lanes], arrived.at[which * (CHUNKS + 1) + chunk]
            )
            copies[which, chunk].start()
    group = lane_group((HALF, LANES))
    for which in range(2):
        copies[which, CHUNKS].wait()
        for block in range(PEERS // 4):
            at = slice(TAIL_AT + block * LANES, TAIL_AT + (block + 1) * LANES)
            tails = [
                sources_ref[which, part, half * HALF : (half + 1) * HALF, at].astype(F32)
                for part in range(2)
                for half in range(2)
            ]
            for quarter in range(4):
                packed = turn(tails[0], -quarter)
                for slot in range(1, 4):
                    packed = jnp.where(group == slot, turn(tails[slot], slot - quarter), packed)
                place, lanes = REVERSED[block * 4 + quarter], slice(which * LANES, (which + 1) * LANES)
                out_ref[place, 4 * OWNED : 4 * OWNED + HALF, lanes] = packed.astype(BF16)
    for chunk in range(CHUNKS):
        for which in range(2):
            copies[which, chunk].wait()
            for peer in range(chunk * peers, (chunk + 1) * peers):
                for part in range(2):
                    row = (which * 2 + part) * OWNED
                    out_ref[REVERSED[peer], row : row + OWNED, :] = sources_ref[
                        which, part, :, peer * MAIN : (peer + 1) * MAIN
                    ]
        places = pl.ds(PEERS - (chunk + 1) * peers, peers)
        copy = pltpu.make_async_copy(out_ref.at[places], out_hbm.at[places], sent.at[chunk])
        copy.start()
        leaving.append(copy)
    for copy in leaving:
        copy.wait()


def main_of(got_ref, which, part):
    at = (which * 2 + part) * OWNED
    return jnp.concatenate([got_ref[place, at : at + OWNED, :] for place in REVERSED], axis=0)


def tails_of(got_ref, which, places):
    lanes = slice(which * LANES, (which + 1) * LANES)
    values = [got_ref[place, 4 * OWNED : 4 * OWNED + HALF, lanes] for place in places]
    return jnp.concatenate(values, axis=0).astype(F32).reshape(PEERS, HALF, LANES)


def unpack_kernel(back_ref, out_ref):
    for peer in range(PEERS):
        for block in range(2):
            at = peer * MAIN + block * LANES
            for part in range(2):
                row = SHARE_ROWS + (block * 2 + part) * OWNED
                out_ref[part, :, at : at + LANES] = back_ref[REVERSED[peer], row : row + OWNED, :]
    group = lane_group((HALF, LANES))
    for block in range(PEERS // 4):
        ends = [back_ref[REVERSED[block * 4 + quarter], SHARE_ROWS + TAIL_ROW : SHARE_ROWS + PIECE_ROWS, :].astype(F32) for quarter in range(4)]
        at = TAIL_AT + block * LANES
        for slot in range(4):
            values = turn(ends[0], -slot)
            for quarter in range(1, 4):
                values = jnp.where(group == quarter, turn(ends[quarter], quarter - slot), values)
            part, half = divmod(slot, 2)
            out_ref[part, half * HALF : (half + 1) * HALF, at : at + LANES] = values.astype(BF16)


def split(values):
    high = values.astype(BF16)
    return high, (values - high.astype(F32)).astype(BF16)


def turn_kernel(ritz_ref, turn_ref):
    real, imag = ritz_ref[0].T, ritz_ref[1].T
    for row, column, block in ((0, 0, real), (0, 1, -imag), (1, 0, imag), (1, 1, real)):
        turn_ref[row * MODES : (row + 1) * MODES, column * MODES : (column + 1) * MODES] = block.astype(BF16)


def split_kernel(ritz_ref, high_ref, low_ref):
    for part in range(2):
        high_ref[part], low_ref[part] = split(ritz_ref[part])


def left_kernel(ritz_ref, left_high_ref, left_low_ref):
    groups = (PEERS, 2, HALF, MODES)
    real, imag = ritz_ref[0].reshape(groups), ritz_ref[1].reshape(groups)
    for core in range(2):
        for part in range(2):
            one, two = (real, imag) if part == 0 else (-imag, real)
            values = jnp.concatenate([side[owner, core] for owner in REVERSED for side in (one, two)], axis=0).T
            rows = slice(part * MODES, (part + 1) * MODES)
            left_high_ref[core, rows, :], left_low_ref[core, rows, :] = split(values)


def rotate_kernel(got_ref, turn_ref, out_ref, stacked):
    packed = tails_of(got_ref, 0, REVERSED)
    for part in range(2):
        rows = slice(part * MODES, (part + 1) * MODES)
        stacked[rows, 0:MAIN] = main_of(got_ref, 0, part)
        ends = jnp.concatenate([turn(packed, -2 * part), turn(packed, -2 * part - 1)], axis=1)
        stacked[rows, MAIN : MAIN + LANES] = ends.reshape(MODES, LANES).astype(BF16)

    owners = HALF_MODES // OWNED
    group = lane_group((owners, HALF, LANES))
    for step in range(2):
        places = REVERSED[step * owners : (step + 1) * owners]
        sent = None
        for part in range(2):
            at = part * MODES + step * HALF_MODES
            rotated = jnp.dot(turn_ref[at : at + HALF_MODES, :], stacked[...], preferred_element_type=F32)
            for block in range(2):
                row = (block * 2 + part) * OWNED
                values = rotated[:, block * LANES : (block + 1) * LANES].astype(BF16)
                for owner, place in enumerate(places):
                    out_ref[place, row : row + OWNED, :] = values[owner * OWNED : (owner + 1) * OWNED, :]
            ends = rotated[:, MAIN : MAIN + LANES].reshape(owners, OWNED, LANES)
            for half in range(2):
                moved = turn(ends[:, half * HALF : (half + 1) * HALF, :], part * 2 + half)
                sent = moved if sent is None else jnp.where(group == part * 2 + half, moved, sent)
        for owner, place in enumerate(places):
            out_ref[place, TAIL_ROW:PIECE_ROWS, :] = sent[owner].astype(BF16)


def share_kernel(other, got_ref, out_ref, left, right):
    core = lax.rem(lax.axis_index("site"), 2)
    half = 1 - core if other else core
    group = lane_group((PEERS, HALF, LANES))

    def side(packed, row_half, sources, signs):
        first, second = (turn(packed, place - 2 * sources[place] - row_half) * signs[place] for place in range(2))
        return jnp.where(group == 0, first, jnp.where(group == 1, second, 0.0))

    packed = tails_of(got_ref, 0, range(PEERS))
    for part in range(2):
        row = pl.multiple_of(part * OWNED + half * HALF, HALF)
        left[:, part * MAIN : (part + 1) * MAIN] = got_ref[:, pl.ds(row, HALF), :].reshape(HALF_MODES, MAIN)
    ends = jnp.where(half == 0, side(packed, 0, (0, 1), (1, 1)), side(packed, 1, (0, 1), (1, 1)))
    left[:, 2 * MAIN : DEPTH] = ends.reshape(HALF_MODES, LANES).astype(BF16)

    packed = tails_of(got_ref, 1, REVERSED)
    for part in range(2):
        sources, signs = ((0, 1), (1, 1)) if part == 0 else ((1, 0), (1, -1))
        for place in range(2):
            values = main_of(got_ref, 1, sources[place])
            right[part, :, place * MAIN : (place + 1) * MAIN] = values if signs[place] > 0 else -values
        ends = jnp.concatenate([side(packed, row_half, sources, signs) for row_half in range(2)], axis=1)
        right[part, :, 2 * MAIN : DEPTH] = ends.reshape(MODES, LANES).astype(BF16)
    for part in range(2):
        share = lax.dot_general(left[...], right[part], NT, preferred_element_type=F32)
        for column in range(4):
            row = (part * 4 + column) * HALF
            values = share[:, column * LANES : (column + 1) * LANES].reshape(PEERS, HALF, LANES)
            out_ref[:, row : row + HALF, :] = values.astype(out_ref.dtype)


def assemble_kernel(kept_ref, taken_ref, turned_ref, out_ref):
    out_ref[:, 0:SHARE_ROWS, :] = (kept_ref[...] + taken_ref[...].astype(F32)).astype(BF16)
    out_ref[:, SHARE_ROWS:, :] = turned_ref[...]


def sum_kernel(back_ref, out_ref):
    total = back_ref[0, 0:SHARE_ROWS, :].astype(F32)
    for peer in range(1, PEERS):
        total += back_ref[peer, 0:SHARE_ROWS, :].astype(F32)
    total = total.astype(BF16)
    for part in range(2):
        for column in range(4):
            at = (part * 4 + column) * HALF
            for copy in range(out_ref.shape[0]):
                out_ref[copy, part * HALF : (part + 1) * HALF, column * LANES : (column + 1) * LANES] = total[
                    at : at + HALF, :
                ]


def total_of(pieces_ref):
    total = pieces_ref[0].astype(F32)
    for peer in range(1, pieces_ref.shape[0]):
        total += pieces_ref[peer].astype(F32)
    return total


def add_kernel(pieces_ref, out_ref):
    total = total_of(pieces_ref).astype(BF16)
    for copy in range(out_ref.shape[0]):
        out_ref[copy] = total


def project_kernel(pieces_ref, high_ref, low_ref, out_ref):
    high, low = split(total_of(pieces_ref))
    both = jnp.concatenate([high, low], axis=0)
    products = []
    for part in range(2):
        first = jnp.dot(both, high_ref[part], preferred_element_type=F32)
        second = jnp.dot(high, low_ref[part], preferred_element_type=F32)
        products.append(first[0:OWNED] + first[OWNED : 2 * OWNED] + second)
    real = products[0][0:HALF] - products[1][HALF:OWNED]
    imag = products[0][HALF:OWNED] + products[1][0:HALF]
    rows = jnp.concatenate([real, imag], axis=0).astype(BF16)
    for copy in range(out_ref.shape[0]):
        out_ref[copy] = rows


def finish_products(half, rows_ref, high_ref, low_ref, here):
    rows = rows_ref[...].reshape(MODES, MODES)
    total = jnp.dot(high_ref[half, here, :], rows, preferred_element_type=F32)
    return total + jnp.dot(low_ref[half, here, :], rows, preferred_element_type=F32)


def finish_own_kernel(rows_ref, high_ref, low_ref, out_ref):
    core = lax.rem(lax.axis_index("site"), 2)
    for part in range(2):
        out_ref[part] = finish_products(core, rows_ref, high_ref, low_ref, pl.ds(part * MODES, MODES))


def finish_other_kernel(rows_ref, high_ref, low_ref, first_ref, back_ref, out_hbm, rotated_hbm, total, rotated, sent):
    core = lax.rem(lax.axis_index("site"), 2)
    copies = []
    for part in range(2):
        for half in range(2):
            rows = pl.ds(half * HALF_MODES, HALF_MODES)
            here = pl.ds(part * MODES + half * HALF_MODES, HALF_MODES)
            total[part, rows, :] = first_ref[part, rows, :] + finish_products(1 - core, rows_ref, high_ref, low_ref, here)
            copy = pltpu.make_async_copy(total.at[part, rows, :], out_hbm.at[part, rows, :], sent.at[part * 2 + half])
            copy.start()
            copies.append(copy)
    unpack_kernel(back_ref, rotated)
    copy = pltpu.make_async_copy(rotated, rotated_hbm, sent.at[4])
    copy.start()
    for done in copies + [copy]:
        done.wait()


def call(kernel, name, outs, *args, flops=0, scratch=(), in_place=False, out_place=False, vmem=16):
    outs = tuple(jax.ShapeDtypeStruct(shape, dtype) for shape, dtype in outs)
    moved = sum(a.size * a.dtype.itemsize for a in args + outs)
    whole = pl.BlockSpec(memory_space=pltpu.VMEM)
    source = pl.BlockSpec(memory_space=pltpu.HBM) if in_place else whole
    target = pl.BlockSpec(memory_space=pltpu.HBM) if out_place else whole
    single = len(outs) == 1
    return pl.pallas_call(
        kernel,
        name=name,
        out_shape=outs[0] if single else outs,
        in_specs=[source] * len(args),
        out_specs=target if single else [target] * len(outs),
        scratch_shapes=list(scratch),
        cost_estimate=pl.CostEstimate(flops=flops, bytes_accessed=moved, transcendentals=0),
        compiler_params=pltpu.CompilerParams(vmem_limit_bytes=vmem * MIB),
    )(*args)


def exchange(pieces, axis, groups=None):
    return lax.all_to_all(pieces, axis, 0, 0, axis_index_groups=groups)


def on_device(site_count, vectors, images, ritz):
    cores, steps = range(2), range(NEAR)
    near_groups = [[[2 * (NEAR * h + z) + c for z in (3,2,1,0)] for h in steps] for c in cores]
    far_groups = [[[2 * (NEAR * h + z) + c for h in (2,1,3,0)] for z in steps] for c in cores]
    swap = [(i, i ^ 1) for i in range(site_count)]
    width = PEERS * MAIN + 4 * LANES
    share = (PEERS, SHARE_ROWS, LANES)
    square = (2 * MODES, 2 * MODES)
    local = [((2, OWNED, width), BF16)]

    packed = call(
        pack_kernel,
        "pack",
        [((PEERS, 4 * OWNED + HALF, MAIN), BF16)],
        vectors,
        images,
        scratch=[
            pltpu.VMEM((2, 2, OWNED, width), BF16),
            pltpu.VMEM((PEERS, 4 * OWNED + HALF, MAIN), BF16),
            pltpu.SemaphoreType.DMA((2 * CHUNKS + 2,)),
            pltpu.SemaphoreType.DMA((CHUNKS,)),
        ],
        in_place=True,
        out_place=True,
        vmem=60,
    )
    packed, ritz = lax.optimization_barrier((packed, ritz))
    factors = (
        call(turn_kernel, "turn_matrix", [(square, BF16)], ritz),
        call(left_kernel, "left_factors", [((2, 2 * MODES, MODES), BF16)] * 2, ritz),
        call(split_kernel, "split_ritz", [(ritz.shape, BF16)] * 2, ritz),
    )
    got, (turn_matrix, left, ritz_split) = lax.optimization_barrier((exchange(packed, "mode", [REVERSED]), factors))

    sides = [pltpu.VMEM((HALF_MODES, DEPTH), BF16), pltpu.VMEM((2, MODES, DEPTH), BF16)]
    given = call(functools.partial(share_kernel, True), "share_given", [(share, BF16)], got, flops=10**9, scratch=sides)
    taken = lax.ppermute(given, "site", swap)
    kept = call(functools.partial(share_kernel, False), "share_kept", [(share, F32)], got, flops=10**9, scratch=sides)
    turned = call(
        rotate_kernel,
        "rotate",
        [((PEERS, PIECE_ROWS, LANES), BF16)],
        got,
        turn_matrix,
        flops=10**9,
        scratch=[pltpu.VMEM((2 * MODES, MAIN + LANES), BF16)],
    )
    sent = call(assemble_kernel, "assemble", [((PEERS, SHARE_ROWS + PIECE_ROWS, LANES), BF16)], kept, taken, turned)
    back = exchange(sent, "mode", [REVERSED])
    summed = call(sum_kernel, "sum_shares", [((NEAR, OWNED, MODES), BF16)], back)
    summed = exchange(summed, "site", far_groups[0] + near_groups[1])
    summed = call(add_kernel, "add_shares", [((NEAR, OWNED, MODES), BF16)], summed)
    summed = exchange(summed, "site", near_groups[0] + far_groups[1])
    rows = call(project_kernel, "project", [((PEERS, OWNED, MODES), BF16)], summed, *ritz_split)
    own = exchange(rows, "mode", [REVERSED])
    other = lax.ppermute(own, "site", swap)
    whole = [((2, MODES, MODES), F32)]
    first = call(finish_own_kernel, "finish_own", whole, own, *left, flops=10**9)
    projected, rotated = call(
        finish_other_kernel,
        "finish_other",
        whole + local,
        other,
        *left,
        first,
        back,
        flops=10**9,
        scratch=[pltpu.VMEM((2, MODES, MODES), F32), pltpu.VMEM(*local[0]), pltpu.SemaphoreType.DMA((5,))],
        out_place=True,
    )
    return rotated, projected


def solution(mesh):
    placed = (P(None, "mode", "site"), P(None, "mode", "site"), P())
    return jax.shard_map(
        functools.partial(on_device, mesh.shape["site"]),
        mesh=mesh,
        in_specs=placed,
        out_specs=(P(None, "mode", "site"), P()),
        check_vma=False,
    )
```

```python
import functools

import jax
import jax.numpy as jnp
from jax import lax
from jax.experimental import pallas as pl
from jax.experimental.pallas import tpu as pltpu
from jax.sharding import PartitionSpec as P

BF16 = jnp.bfloat16
F32 = jnp.float32
LANES = 128
MIB = 1024 * 1024

PEERS = 16
OWNED = 32
HALF = OWNED // 2
MODES = PEERS * OWNED
HALF_MODES = MODES // 2
MAIN = 2 * LANES
QUARTER = LANES // 4
TAIL_AT = PEERS * MAIN
TAIL_ROW = 4 * OWNED
PIECE_ROWS = TAIL_ROW + HALF
DEPTH = 2 * MAIN + LANES
SHARE_ROWS = 8 * HALF
CHUNKS = 4
NEAR = 4

REVERSED = list(range(PEERS))[::-1]

NT = (((1,), (1,)), ((), ()))


def lane_group(shape):
    return lax.broadcasted_iota(jnp.int32, shape, len(shape) - 1) // QUARTER


def turn(values, groups):
    shift = groups % 4 * QUARTER
    return pltpu.roll(values, shift, len(values.shape) - 1) if shift else values


def pack_kernel(vectors_hbm, images_hbm, out_hbm, sources_ref, out_ref, arrived, sent):
    peers = PEERS // CHUNKS
    copies, leaving = {}, []
    for chunk in (CHUNKS, *range(CHUNKS)):
        for which, source in enumerate((vectors_hbm, images_hbm)):
            lanes = pl.ds(chunk * peers * MAIN, peers * MAIN if chunk < CHUNKS else 4 * LANES)
            copies[which, chunk] = pltpu.make_async_copy(
                source.at[:, :, lanes], sources_ref.at[which, :, :, lanes], arrived.at[which * (CHUNKS + 1) + chunk]
            )
            copies[which, chunk].start()
    group = lane_group((HALF, LANES))
    for which in range(2):
        copies[which, CHUNKS].wait()
        for block in range(PEERS // 4):
            at = slice(TAIL_AT + block * LANES, TAIL_AT + (block + 1) * LANES)
            tails = [
                sources_ref[which, part, half * HALF : (half + 1) * HALF, at].astype(F32)
                for part in range(2)
                for half in range(2)
            ]
            for quarter in range(4):
                packed = turn(tails[0], -quarter)
                for slot in range(1, 4):
                    packed = jnp.where(group == slot, turn(tails[slot], slot - quarter), packed)
                place, lanes = REVERSED[block * 4 + quarter], slice(which * LANES, (which + 1) * LANES)
                out_ref[place, 4 * OWNED : 4 * OWNED + HALF, lanes] = packed.astype(BF16)
    for chunk in range(CHUNKS):
        for which in range(2):
            copies[which, chunk].wait()
            for peer in range(chunk * peers, (chunk + 1) * peers):
                for part in range(2):
                    row = (which * 2 + part) * OWNED
                    out_ref[REVERSED[peer], row : row + OWNED, :] = sources_ref[
                        which, part, :, peer * MAIN : (peer + 1) * MAIN
                    ]
        places = pl.ds(PEERS - (chunk + 1) * peers, peers)
        copy = pltpu.make_async_copy(out_ref.at[places], out_hbm.at[places], sent.at[chunk])
        copy.start()
        leaving.append(copy)
    for copy in leaving:
        copy.wait()


def main_of(got_ref, which, part):
    at = (which * 2 + part) * OWNED
    return jnp.concatenate([got_ref[place, at : at + OWNED, :] for place in REVERSED], axis=0)


def tails_of(got_ref, which, places):
    lanes = slice(which * LANES, (which + 1) * LANES)
    values = [got_ref[place, 4 * OWNED : 4 * OWNED + HALF, lanes] for place in places]
    return jnp.concatenate(values, axis=0).astype(F32).reshape(PEERS, HALF, LANES)


def unpack_kernel(back_ref, out_ref):
    for peer in range(PEERS):
        for block in range(2):
            at = peer * MAIN + block * LANES
            for part in range(2):
                row = SHARE_ROWS + (block * 2 + part) * OWNED
                out_ref[part, :, at : at + LANES] = back_ref[REVERSED[peer], row : row + OWNED, :]
    group = lane_group((HALF, LANES))
    for block in range(PEERS // 4):
        ends = [back_ref[REVERSED[block * 4 + quarter], SHARE_ROWS + TAIL_ROW : SHARE_ROWS + PIECE_ROWS, :].astype(F32) for quarter in range(4)]
        at = TAIL_AT + block * LANES
        for slot in range(4):
            values = turn(ends[0], -slot)
            for quarter in range(1, 4):
                values = jnp.where(group == quarter, turn(ends[quarter], quarter - slot), values)
            part, half = divmod(slot, 2)
            out_ref[part, half * HALF : (half + 1) * HALF, at : at + LANES] = values.astype(BF16)


def split(values):
    high = values.astype(BF16)
    return high, (values - high.astype(F32)).astype(BF16)


def turn_kernel(ritz_ref, turn_ref):
    real, imag = ritz_ref[0].T, ritz_ref[1].T
    for row, column, block in ((0, 0, real), (0, 1, -imag), (1, 0, imag), (1, 1, real)):
        turn_ref[row * MODES : (row + 1) * MODES, column * MODES : (column + 1) * MODES] = block.astype(BF16)


def split_kernel(ritz_ref, high_ref, low_ref):
    for part in range(2):
        high_ref[part], low_ref[part] = split(ritz_ref[part])


def left_kernel(ritz_ref, left_high_ref, left_low_ref):
    groups = (PEERS, 2, HALF, MODES)
    real, imag = ritz_ref[0].reshape(groups), ritz_ref[1].reshape(groups)
    for core in range(2):
        for part in range(2):
            one, two = (real, imag) if part == 0 else (-imag, real)
            values = jnp.concatenate([side[owner, core] for owner in REVERSED for side in (one, two)], axis=0).T
            rows = slice(part * MODES, (part + 1) * MODES)
            left_high_ref[core, rows, :], left_low_ref[core, rows, :] = split(values)


def rotate_kernel(got_ref, turn_ref, out_ref, stacked):
    packed = tails_of(got_ref, 0, REVERSED)
    for part in range(2):
        rows = slice(part * MODES, (part + 1) * MODES)
        stacked[rows, 0:MAIN] = main_of(got_ref, 0, part)
        ends = jnp.concatenate([turn(packed, -2 * part), turn(packed, -2 * part - 1)], axis=1)
        stacked[rows, MAIN : MAIN + LANES] = ends.reshape(MODES, LANES).astype(BF16)

    owners = HALF_MODES // OWNED
    group = lane_group((owners, HALF, LANES))
    for step in range(2):
        places = REVERSED[step * owners : (step + 1) * owners]
        sent = None
        for part in range(2):
            at = part * MODES + step * HALF_MODES
            rotated = jnp.dot(turn_ref[at : at + HALF_MODES, :], stacked[...], preferred_element_type=F32)
            for block in range(2):
                row = (block * 2 + part) * OWNED
                values = rotated[:, block * LANES : (block + 1) * LANES].astype(BF16)
                for owner, place in enumerate(places):
                    out_ref[place, row : row + OWNED, :] = values[owner * OWNED : (owner + 1) * OWNED, :]
            ends = rotated[:, MAIN : MAIN + LANES].reshape(owners, OWNED, LANES)
            for half in range(2):
                moved = turn(ends[:, half * HALF : (half + 1) * HALF, :], part * 2 + half)
                sent = moved if sent is None else jnp.where(group == part * 2 + half, moved, sent)
        for owner, place in enumerate(places):
            out_ref[place, TAIL_ROW:PIECE_ROWS, :] = sent[owner].astype(BF16)


def share_kernel(other, *refs):
    got_ref, out_ref, right, left = refs if other else (refs[0], refs[2], refs[1], refs[3])
    core = lax.rem(lax.axis_index("site"), 2)
    half = 1 - core if other else core
    group = lane_group((PEERS, HALF, LANES))

    def side(packed, row_half, sources, signs):
        first, second = (turn(packed, place - 2 * sources[place] - row_half) * signs[place] for place in range(2))
        return jnp.where(group == 0, first, jnp.where(group == 1, second, 0.0))

    packed = tails_of(got_ref, 0, range(PEERS))
    for part in range(2):
        row = pl.multiple_of(part * OWNED + half * HALF, HALF)
        left[:, part * MAIN : (part + 1) * MAIN] = got_ref[:, pl.ds(row, HALF), :].reshape(HALF_MODES, MAIN)
    ends = jnp.where(half == 0, side(packed, 0, (0, 1), (1, 1)), side(packed, 1, (0, 1), (1, 1)))
    left[:, 2 * MAIN : DEPTH] = ends.reshape(HALF_MODES, LANES).astype(BF16)

    packed = tails_of(got_ref, 1, REVERSED) if other else None
    for part in range(2 if other else 0):
        sources, signs = ((0, 1), (1, 1)) if part == 0 else ((1, 0), (1, -1))
        for place in range(2):
            values = main_of(got_ref, 1, sources[place])
            right[part, :, place * MAIN : (place + 1) * MAIN] = values if signs[place] > 0 else -values
        ends = jnp.concatenate([side(packed, row_half, sources, signs) for row_half in range(2)], axis=1)
        right[part, :, 2 * MAIN : DEPTH] = ends.reshape(MODES, LANES).astype(BF16)
    for part in range(2):
        share = lax.dot_general(left[...], right[part], NT, preferred_element_type=F32)
        for column in range(4):
            row = (part * 4 + column) * HALF
            values = share[:, column * LANES : (column + 1) * LANES].reshape(PEERS, HALF, LANES)
            out_ref[:, row : row + HALF, :] = values.astype(out_ref.dtype)


def assemble_kernel(kept_ref, taken_ref, turned_ref, out_ref):
    out_ref[:, 0:SHARE_ROWS, :] = (kept_ref[...] + taken_ref[...].astype(F32)).astype(BF16)
    out_ref[:, SHARE_ROWS:, :] = turned_ref[...]


def sum_kernel(back_ref, out_ref):
    total = back_ref[0, 0:SHARE_ROWS, :].astype(F32)
    for peer in range(1, PEERS):
        total += back_ref[peer, 0:SHARE_ROWS, :].astype(F32)
    total = total.astype(BF16)
    for part in range(2):
        for column in range(4):
            at = (part * 4 + column) * HALF
            for copy in range(out_ref.shape[0]):
                out_ref[copy, part * HALF : (part + 1) * HALF, column * LANES : (column + 1) * LANES] = total[
                    at : at + HALF, :
                ]


def total_of(pieces_ref):
    total = pieces_ref[0].astype(F32)
    for peer in range(1, pieces_ref.shape[0]):
        total += pieces_ref[peer].astype(F32)
    return total


def add_kernel(pieces_ref, out_ref):
    total = total_of(pieces_ref).astype(BF16)
    for copy in range(out_ref.shape[0]):
        out_ref[copy] = total


def project_kernel(pieces_ref, high_ref, low_ref, out_ref):
    high, low = split(total_of(pieces_ref))
    both = jnp.concatenate([high, low], axis=0)
    products = []
    for part in range(2):
        first = jnp.dot(both, high_ref[part], preferred_element_type=F32)
        second = jnp.dot(high, low_ref[part], preferred_element_type=F32)
        products.append(first[0:OWNED] + first[OWNED : 2 * OWNED] + second)
    real = products[0][0:HALF] - products[1][HALF:OWNED]
    imag = products[0][HALF:OWNED] + products[1][0:HALF]
    rows = jnp.concatenate([real, imag], axis=0).astype(BF16)
    for copy in range(out_ref.shape[0]):
        out_ref[copy] = rows


def finish_products(half, rows_ref, high_ref, low_ref, here):
    rows = rows_ref[...].reshape(MODES, MODES)
    total = jnp.dot(high_ref[half, here, :], rows, preferred_element_type=F32)
    return total + jnp.dot(low_ref[half, here, :], rows, preferred_element_type=F32)


def finish_own_kernel(rows_ref, high_ref, low_ref, out_ref):
    core = lax.rem(lax.axis_index("site"), 2)
    for part in range(2):
        out_ref[part] = finish_products(core, rows_ref, high_ref, low_ref, pl.ds(part * MODES, MODES))


def finish_other_kernel(rows_ref, high_ref, low_ref, first_ref, back_ref, out_hbm, rotated_hbm, total, rotated, sent):
    core = lax.rem(lax.axis_index("site"), 2)
    copies = []
    for part in range(2):
        for half in range(2):
            rows = pl.ds(half * HALF_MODES, HALF_MODES)
            here = pl.ds(part * MODES + half * HALF_MODES, HALF_MODES)
            total[part, rows, :] = first_ref[part, rows, :] + finish_products(1 - core, rows_ref, high_ref, low_ref, here)
            copy = pltpu.make_async_copy(total.at[part, rows, :], out_hbm.at[part, rows, :], sent.at[part * 2 + half])
            copy.start()
            copies.append(copy)
    unpack_kernel(back_ref, rotated)
    copy = pltpu.make_async_copy(rotated, rotated_hbm, sent.at[4])
    copy.start()
    for done in copies + [copy]:
        done.wait()


def call(kernel, name, outs, *args, flops=0, scratch=(), in_place=False, out_place=False, vmem=16):
    outs = tuple(jax.ShapeDtypeStruct(shape, dtype) for shape, dtype in outs)
    moved = sum(a.size * a.dtype.itemsize for a in args + outs)
    whole = pl.BlockSpec(memory_space=pltpu.VMEM)
    source = pl.BlockSpec(memory_space=pltpu.HBM) if in_place else whole
    target = pl.BlockSpec(memory_space=pltpu.HBM) if out_place else whole
    single = len(outs) == 1
    return pl.pallas_call(
        kernel,
        name=name,
        out_shape=outs[0] if single else outs,
        in_specs=[source] * len(args),
        out_specs=target if single else [target] * len(outs),
        scratch_shapes=list(scratch),
        cost_estimate=pl.CostEstimate(flops=flops, bytes_accessed=moved, transcendentals=0),
        compiler_params=pltpu.CompilerParams(vmem_limit_bytes=vmem * MIB),
    )(*args)


def exchange(pieces, axis, groups=None):
    return lax.all_to_all(pieces, axis, 0, 0, axis_index_groups=groups)


def on_device(site_count, vectors, images, ritz):
    cores, steps = range(2), range(NEAR)
    near_groups = [[[2 * (NEAR * h + z) + c for z in (3,2,1,0)] for h in steps] for c in cores]
    far_groups = [[[2 * (NEAR * h + z) + c for h in (2,1,3,0)] for z in steps] for c in cores]
    swap = [(i, i ^ 1) for i in range(site_count)]
    width = PEERS * MAIN + 4 * LANES
    share = (PEERS, SHARE_ROWS, LANES)
    square = (2 * MODES, 2 * MODES)
    local = [((2, OWNED, width), BF16)]

    packed = call(
        pack_kernel,
        "pack",
        [((PEERS, 4 * OWNED + HALF, MAIN), BF16)],
        vectors,
        images,
        scratch=[
            pltpu.VMEM((2, 2, OWNED, width), BF16),
            pltpu.VMEM((PEERS, 4 * OWNED + HALF, MAIN), BF16),
            pltpu.SemaphoreType.DMA((2 * CHUNKS + 2,)),
            pltpu.SemaphoreType.DMA((CHUNKS,)),
        ],
        in_place=True,
        out_place=True,
        vmem=60,
    )
    packed, ritz = lax.optimization_barrier((packed, ritz))
    factors = (
        call(turn_kernel, "turn_matrix", [(square, BF16)], ritz),
        call(left_kernel, "left_factors", [((2, 2 * MODES, MODES), BF16)] * 2, ritz),
        call(split_kernel, "split_ritz", [(ritz.shape, BF16)] * 2, ritz),
    )
    got, (turn_matrix, left, ritz_split) = lax.optimization_barrier((exchange(packed, "mode", [REVERSED]), factors))

    side = [pltpu.VMEM((HALF_MODES, DEPTH), BF16)]
    factor = ((2, MODES, DEPTH), BF16)
    given, right = call(
        functools.partial(share_kernel, True), "share_given", [(share, BF16), factor], got, flops=10**9, scratch=side
    )
    taken = lax.ppermute(given, "site", swap)
    kept = call(
        functools.partial(share_kernel, False), "share_kept", [(share, F32)], got, right, flops=10**9, scratch=side
    )
    turned = call(
        rotate_kernel,
        "rotate",
        [((PEERS, PIECE_ROWS, LANES), BF16)],
        got,
        turn_matrix,
        flops=10**9,
        scratch=[pltpu.VMEM((2 * MODES, MAIN + LANES), BF16)],
    )
    sent = call(assemble_kernel, "assemble", [((PEERS, SHARE_ROWS + PIECE_ROWS, LANES), BF16)], kept, taken, turned)
    back = exchange(sent, "mode", [REVERSED])
    summed = call(sum_kernel, "sum_shares", [((NEAR, OWNED, MODES), BF16)], back)
    summed = exchange(summed, "site", far_groups[0] + near_groups[1])
    summed = call(add_kernel, "add_shares", [((NEAR, OWNED, MODES), BF16)], summed)
    summed = exchange(summed, "site", near_groups[0] + far_groups[1])
    rows = call(project_kernel, "project", [((PEERS, OWNED, MODES), BF16)], summed, *ritz_split)
    own = exchange(rows, "mode", [REVERSED])
    other = lax.ppermute(own, "site", swap)
    whole = [((2, MODES, MODES), F32)]
    first = call(finish_own_kernel, "finish_own", whole, own, *left, flops=10**9)
    projected, rotated = call(
        finish_other_kernel,
        "finish_other",
        whole + local,
        other,
        *left,
        first,
        back,
        flops=10**9,
        scratch=[pltpu.VMEM((2, MODES, MODES), F32), pltpu.VMEM(*local[0]), pltpu.SemaphoreType.DMA((5,))],
        out_place=True,
    )
    return rotated, projected


def solution(mesh):
    placed = (P(None, "mode", "site"), P(None, "mode", "site"), P())
    return jax.shard_map(
        functools.partial(on_device, mesh.shape["site"]),
        mesh=mesh,
        in_specs=placed,
        out_specs=(P(None, "mode", "site"), P()),
        check_vma=False,
    )
```

```python
import functools

import jax
import jax.numpy as jnp
from jax import lax
from jax.experimental import pallas as pl
from jax.experimental.pallas import tpu as pltpu
from jax.sharding import PartitionSpec as P

BF16 = jnp.bfloat16
F32 = jnp.float32
LANES = 128
MIB = 1024 * 1024

PEERS = 16
OWNED = 32
HALF = OWNED // 2
MODES = PEERS * OWNED
HALF_MODES = MODES // 2
MAIN = 2 * LANES
QUARTER = LANES // 4
TAIL_AT = PEERS * MAIN
TAIL_ROW = 4 * OWNED
PIECE_ROWS = TAIL_ROW + HALF
DEPTH = 2 * MAIN + LANES
SHARE_ROWS = 8 * HALF
CHUNKS = 4
NEAR = 4

REVERSED = list(range(PEERS))[::-1]

NT = (((1,), (1,)), ((), ()))


def lane_group(shape):
    return lax.broadcasted_iota(jnp.int32, shape, len(shape) - 1) // QUARTER


def turn(values, groups):
    shift = groups % 4 * QUARTER
    return pltpu.roll(values, shift, len(values.shape) - 1) if shift else values


def pack_kernel(vectors_hbm, images_hbm, out_hbm, sources_ref, out_ref, arrived, sent):
    peers = PEERS // CHUNKS
    copies, leaving = {}, []
    for chunk in (CHUNKS, *range(CHUNKS)):
        for which, source in enumerate((vectors_hbm, images_hbm)):
            lanes = pl.ds(chunk * peers * MAIN, peers * MAIN if chunk < CHUNKS else 4 * LANES)
            copies[which, chunk] = pltpu.make_async_copy(
                source.at[:, :, lanes], sources_ref.at[which, :, :, lanes], arrived.at[which * (CHUNKS + 1) + chunk]
            )
            copies[which, chunk].start()
    group = lane_group((HALF, LANES))
    for which in range(2):
        copies[which, CHUNKS].wait()
        for block in range(PEERS // 4):
            at = slice(TAIL_AT + block * LANES, TAIL_AT + (block + 1) * LANES)
            tails = [
                sources_ref[which, part, half * HALF : (half + 1) * HALF, at].astype(F32)
                for part in range(2)
                for half in range(2)
            ]
            for quarter in range(4):
                packed = turn(tails[0], -quarter)
                for slot in range(1, 4):
                    packed = jnp.where(group == slot, turn(tails[slot], slot - quarter), packed)
                place, lanes = REVERSED[block * 4 + quarter], slice(which * LANES, (which + 1) * LANES)
                out_ref[place, 4 * OWNED : 4 * OWNED + HALF, lanes] = packed.astype(BF16)
    for chunk in range(CHUNKS):
        for which in range(2):
            copies[which, chunk].wait()
            for peer in range(chunk * peers, (chunk + 1) * peers):
                for part in range(2):
                    row = (which * 2 + part) * OWNED
                    out_ref[REVERSED[peer], row : row + OWNED, :] = sources_ref[
                        which, part, :, peer * MAIN : (peer + 1) * MAIN
                    ]
        places = pl.ds(PEERS - (chunk + 1) * peers, peers)
        copy = pltpu.make_async_copy(out_ref.at[places], out_hbm.at[places], sent.at[chunk])
        copy.start()
        leaving.append(copy)
    for copy in leaving:
        copy.wait()


def main_of(got_ref, which, part):
    at = (which * 2 + part) * OWNED
    return jnp.concatenate([got_ref[place, at : at + OWNED, :] for place in REVERSED], axis=0)


def tails_of(got_ref, which, places):
    lanes = slice(which * LANES, (which + 1) * LANES)
    values = [got_ref[place, 4 * OWNED : 4 * OWNED + HALF, lanes] for place in places]
    return jnp.concatenate(values, axis=0).astype(F32).reshape(PEERS, HALF, LANES)


def unpack_kernel(back_ref, out_ref):
    for peer in range(PEERS):
        for block in range(2):
            at = peer * MAIN + block * LANES
            for part in range(2):
                row = SHARE_ROWS + (block * 2 + part) * OWNED
                out_ref[part, :, at : at + LANES] = back_ref[REVERSED[peer], row : row + OWNED, :]
    group = lane_group((HALF, LANES))
    for block in range(PEERS // 4):
        ends = [back_ref[REVERSED[block * 4 + quarter], SHARE_ROWS + TAIL_ROW : SHARE_ROWS + PIECE_ROWS, :].astype(F32) for quarter in range(4)]
        at = TAIL_AT + block * LANES
        for slot in range(4):
            values = turn(ends[0], -slot)
            for quarter in range(1, 4):
                values = jnp.where(group == quarter, turn(ends[quarter], quarter - slot), values)
            part, half = divmod(slot, 2)
            out_ref[part, half * HALF : (half + 1) * HALF, at : at + LANES] = values.astype(BF16)


def split(values):
    high = values.astype(BF16)
    return high, (values - high.astype(F32)).astype(BF16)


def turn_kernel(ritz_ref, turn_ref):
    real, imag = ritz_ref[0].T, ritz_ref[1].T
    for row, column, block in ((0, 0, real), (0, 1, -imag), (1, 0, imag), (1, 1, real)):
        turn_ref[row * MODES : (row + 1) * MODES, column * MODES : (column + 1) * MODES] = block.astype(BF16)


def split_kernel(ritz_ref, high_ref, low_ref):
    for part in range(2):
        high_ref[part], low_ref[part] = split(ritz_ref[part])


def left_kernel(ritz_ref, left_high_ref, left_low_ref):
    groups = (PEERS, 2, HALF, MODES)
    real, imag = ritz_ref[0].reshape(groups), ritz_ref[1].reshape(groups)
    for core in range(2):
        for part in range(2):
            one, two = (real, imag) if part == 0 else (-imag, real)
            values = jnp.concatenate([side[owner, core] for owner in REVERSED for side in (one, two)], axis=0).T
            rows = slice(part * MODES, (part + 1) * MODES)
            left_high_ref[core, rows, :], left_low_ref[core, rows, :] = split(values)


def rotate_kernel(got_ref, turn_ref, out_ref, stacked):
    packed = tails_of(got_ref, 0, REVERSED)
    for part in range(2):
        rows = slice(part * MODES, (part + 1) * MODES)
        stacked[rows, 0:MAIN] = main_of(got_ref, 0, part)
        ends = jnp.concatenate([turn(packed, -2 * part), turn(packed, -2 * part - 1)], axis=1)
        stacked[rows, MAIN : MAIN + LANES] = ends.reshape(MODES, LANES).astype(BF16)

    owners = HALF_MODES // OWNED
    group = lane_group((owners, HALF, LANES))
    for step in range(2):
        places = REVERSED[step * owners : (step + 1) * owners]
        sent = None
        for part in range(2):
            at = part * MODES + step * HALF_MODES
            rotated = jnp.dot(turn_ref[at : at + HALF_MODES, :], stacked[...], preferred_element_type=F32)
            for block in range(2):
                row = (block * 2 + part) * OWNED
                values = rotated[:, block * LANES : (block + 1) * LANES].astype(BF16)
                for owner, place in enumerate(places):
                    out_ref[place, row : row + OWNED, :] = values[owner * OWNED : (owner + 1) * OWNED, :]
            ends = rotated[:, MAIN : MAIN + LANES].reshape(owners, OWNED, LANES)
            for half in range(2):
                moved = turn(ends[:, half * HALF : (half + 1) * HALF, :], part * 2 + half)
                sent = moved if sent is None else jnp.where(group == part * 2 + half, moved, sent)
        for owner, place in enumerate(places):
            out_ref[place, TAIL_ROW:PIECE_ROWS, :] = sent[owner].astype(BF16)


def share_kernel(other, *refs):
    got_ref, out_ref, right, left = refs if other else (refs[0], refs[2], refs[1], refs[3])
    core = lax.rem(lax.axis_index("site"), 2)
    half = 1 - core if other else core
    group = lane_group((PEERS, HALF, LANES))

    def side(packed, row_half, sources, signs):
        first, second = (turn(packed, place - 2 * sources[place] - row_half) * signs[place] for place in range(2))
        return jnp.where(group == 0, first, jnp.where(group == 1, second, 0.0))

    packed = tails_of(got_ref, 0, range(PEERS))
    for part in range(2):
        row = pl.multiple_of(part * OWNED + half * HALF, HALF)
        left[:, part * MAIN : (part + 1) * MAIN] = got_ref[:, pl.ds(row, HALF), :].reshape(HALF_MODES, MAIN)
    ends = jnp.where(half == 0, side(packed, 0, (0, 1), (1, 1)), side(packed, 1, (0, 1), (1, 1)))
    left[:, 2 * MAIN : DEPTH] = ends.reshape(HALF_MODES, LANES).astype(BF16)

    packed = tails_of(got_ref, 1, REVERSED) if other else None
    for part in range(2 if other else 0):
        sources, signs = ((0, 1), (1, 1)) if part == 0 else ((1, 0), (1, -1))
        for place in range(2):
            values = main_of(got_ref, 1, sources[place])
            right[part, :, place * MAIN : (place + 1) * MAIN] = values if signs[place] > 0 else -values
        ends = jnp.concatenate([side(packed, row_half, sources, signs) for row_half in range(2)], axis=1)
        right[part, :, 2 * MAIN : DEPTH] = ends.reshape(MODES, LANES).astype(BF16)
    for part in range(2):
        share = lax.dot_general(left[...], right[part], NT, preferred_element_type=F32)
        for column in range(4):
            row = (part * 4 + column) * HALF
            values = share[:, column * LANES : (column + 1) * LANES].reshape(PEERS, HALF, LANES)
            out_ref[:, row : row + HALF, :] = values.astype(out_ref.dtype)


def assemble_kernel(kept_ref, taken_ref, turned_ref, out_ref):
    out_ref[:, 0:SHARE_ROWS, :] = (kept_ref[...] + taken_ref[...].astype(F32)).astype(BF16)
    out_ref[:, SHARE_ROWS:, :] = turned_ref[...]


def sum_kernel(back_ref, out_ref):
    total = back_ref[0, 0:SHARE_ROWS, :].astype(F32)
    for peer in range(1, PEERS):
        total += back_ref[peer, 0:SHARE_ROWS, :].astype(F32)
    total = total.astype(BF16)
    for part in range(2):
        for column in range(4):
            at = (part * 4 + column) * HALF
            for copy in range(out_ref.shape[0]):
                out_ref[copy, part * HALF : (part + 1) * HALF, column * LANES : (column + 1) * LANES] = total[
                    at : at + HALF, :
                ]


def total_of(pieces_ref):
    total = pieces_ref[0].astype(F32)
    for peer in range(1, pieces_ref.shape[0]):
        total += pieces_ref[peer].astype(F32)
    return total


def add_kernel(pieces_ref, out_ref):
    total = total_of(pieces_ref).astype(BF16)
    for copy in range(out_ref.shape[0]):
        out_ref[copy] = total


def project_kernel(pieces_ref, high_ref, low_ref, out_ref):
    high, low = split(total_of(pieces_ref))
    both = jnp.concatenate([high, low], axis=0)
    products = []
    for part in range(2):
        first = jnp.dot(both, high_ref[part], preferred_element_type=F32)
        second = jnp.dot(high, low_ref[part], preferred_element_type=F32)
        products.append(first[0:OWNED] + first[OWNED : 2 * OWNED] + second)
    real = products[0][0:HALF] - products[1][HALF:OWNED]
    imag = products[0][HALF:OWNED] + products[1][0:HALF]
    rows = jnp.concatenate([real, imag], axis=0).astype(BF16)
    for copy in range(out_ref.shape[0]):
        out_ref[copy] = rows


def finish_products(half, rows_ref, high_ref, low_ref, here):
    rows = rows_ref[...].reshape(MODES, MODES)
    total = jnp.dot(high_ref[half, here, :], rows, preferred_element_type=F32)
    return total + jnp.dot(low_ref[half, here, :], rows, preferred_element_type=F32)


def finish_own_kernel(rows_ref, high_ref, low_ref, out_ref):
    core = lax.rem(lax.axis_index("site"), 2)
    for part in range(2):
        out_ref[part] = finish_products(core, rows_ref, high_ref, low_ref, pl.ds(part * MODES, MODES))


def finish_other_kernel(rows_ref, high_ref, low_ref, first_ref, back_ref, out_hbm, rotated_hbm, total, rotated, sent):
    core = lax.rem(lax.axis_index("site"), 2)
    unpack_kernel(back_ref, rotated)
    copies = [pltpu.make_async_copy(rotated, rotated_hbm, sent.at[4])]
    copies[0].start()
    for part in range(2):
        for half in range(2):
            rows = pl.ds(half * HALF_MODES, HALF_MODES)
            here = pl.ds(part * MODES + half * HALF_MODES, HALF_MODES)
            total[part, rows, :] = first_ref[part, rows, :] + finish_products(1 - core, rows_ref, high_ref, low_ref, here)
            copy = pltpu.make_async_copy(total.at[part, rows, :], out_hbm.at[part, rows, :], sent.at[part * 2 + half])
            copy.start()
            copies.append(copy)
    for copy in copies:
        copy.wait()


def call(kernel, name, outs, *args, flops=0, scratch=(), in_place=False, out_place=False, vmem=16):
    outs = tuple(jax.ShapeDtypeStruct(shape, dtype) for shape, dtype in outs)
    moved = sum(a.size * a.dtype.itemsize for a in args + outs)
    whole = pl.BlockSpec(memory_space=pltpu.VMEM)
    source = pl.BlockSpec(memory_space=pltpu.HBM) if in_place else whole
    target = pl.BlockSpec(memory_space=pltpu.HBM) if out_place else whole
    single = len(outs) == 1
    return pl.pallas_call(
        kernel,
        name=name,
        out_shape=outs[0] if single else outs,
        in_specs=[source] * len(args),
        out_specs=target if single else [target] * len(outs),
        scratch_shapes=list(scratch),
        cost_estimate=pl.CostEstimate(flops=flops, bytes_accessed=moved, transcendentals=0),
        compiler_params=pltpu.CompilerParams(vmem_limit_bytes=vmem * MIB),
    )(*args)


def exchange(pieces, axis, groups=None):
    return lax.all_to_all(pieces, axis, 0, 0, axis_index_groups=groups)


def on_device(site_count, vectors, images, ritz):
    cores, steps = range(2), range(NEAR)
    near_groups = [[[2 * (NEAR * h + z) + c for z in (3,2,1,0)] for h in steps] for c in cores]
    far_groups = [[[2 * (NEAR * h + z) + c for h in (2,1,3,0)] for z in steps] for c in cores]
    swap = [(i, i ^ 1) for i in range(site_count)]
    width = PEERS * MAIN + 4 * LANES
    share = (PEERS, SHARE_ROWS, LANES)
    square = (2 * MODES, 2 * MODES)
    local = [((2, OWNED, width), BF16)]

    packed = call(
        pack_kernel,
        "pack",
        [((PEERS, 4 * OWNED + HALF, MAIN), BF16)],
        vectors,
        images,
        scratch=[
            pltpu.VMEM((2, 2, OWNED, width), BF16),
            pltpu.VMEM((PEERS, 4 * OWNED + HALF, MAIN), BF16),
            pltpu.SemaphoreType.DMA((2 * CHUNKS + 2,)),
            pltpu.SemaphoreType.DMA((CHUNKS,)),
        ],
        in_place=True,
        out_place=True,
        vmem=60,
    )
    packed, ritz = lax.optimization_barrier((packed, ritz))
    factors = (
        call(turn_kernel, "turn_matrix", [(square, BF16)], ritz),
        call(left_kernel, "left_factors", [((2, 2 * MODES, MODES), BF16)] * 2, ritz),
        call(split_kernel, "split_ritz", [(ritz.shape, BF16)] * 2, ritz),
    )
    got, (turn_matrix, left, ritz_split) = lax.optimization_barrier((exchange(packed, "mode", [REVERSED]), factors))

    side = [pltpu.VMEM((HALF_MODES, DEPTH), BF16)]
    factor = ((2, MODES, DEPTH), BF16)
    given, right = call(
        functools.partial(share_kernel, True), "share_given", [(share, BF16), factor], got, flops=10**9, scratch=side
    )
    taken = lax.ppermute(given, "site", swap)
    kept = call(
        functools.partial(share_kernel, False), "share_kept", [(share, F32)], got, right, flops=10**9, scratch=side
    )
    turned = call(
        rotate_kernel,
        "rotate",
        [((PEERS, PIECE_ROWS, LANES), BF16)],
        got,
        turn_matrix,
        flops=10**9,
        scratch=[pltpu.VMEM((2 * MODES, MAIN + LANES), BF16)],
    )
    sent = call(assemble_kernel, "assemble", [((PEERS, SHARE_ROWS + PIECE_ROWS, LANES), BF16)], kept, taken, turned)
    back = exchange(sent, "mode", [REVERSED])
    summed = call(sum_kernel, "sum_shares", [((NEAR, OWNED, MODES), BF16)], back)
    summed = exchange(summed, "site", far_groups[0] + near_groups[1])
    summed = call(add_kernel, "add_shares", [((NEAR, OWNED, MODES), BF16)], summed)
    summed = exchange(summed, "site", near_groups[0] + far_groups[1])
    rows = call(project_kernel, "project", [((PEERS, OWNED, MODES), BF16)], summed, *ritz_split)
    own = exchange(rows, "mode", [REVERSED])
    other = lax.ppermute(own, "site", swap)
    whole = [((2, MODES, MODES), F32)]
    first = call(finish_own_kernel, "finish_own", whole, own, *left, flops=10**9)
    projected, rotated = call(
        finish_other_kernel,
        "finish_other",
        whole + local,
        other,
        *left,
        first,
        back,
        flops=10**9,
        scratch=[pltpu.VMEM((2, MODES, MODES), F32), pltpu.VMEM(*local[0]), pltpu.SemaphoreType.DMA((5,))],
        out_place=True,
    )
    return rotated, projected


def solution(mesh):
    placed = (P(None, "mode", "site"), P(None, "mode", "site"), P())
    return jax.shard_map(
        functools.partial(on_device, mesh.shape["site"]),
        mesh=mesh,
        in_specs=placed,
        out_specs=(P(None, "mode", "site"), P()),
        check_vma=False,
    )
```
